256 devices in a mesh: tm: 16 (over z, core), space: 16 (over x, y).
Axes of the slice: x: 4, y: 4, z: 8, core: 2. Of those that a mesh axis runs over, the one named last changes fastest.
Arguments:
- latent: bfloat16 [2, 32, 896, 1152], P(None, 'tm', 'space'), may hold values from -6 to 6
- upstream: bfloat16 [2, 32, 896, 1152], P(None, 'tm', 'space'), may hold values from -6 to 6
- modulation: float32 [2, 6, 1152], replicated, may hold values from -3 to 3
- spatial_qkv: bfloat16 [1152, 3456], P('space'), may hold values from -0.1875 to 0.1875
- spatial_out: bfloat16 [1152, 1152], P('space'), may hold values from -0.1875 to 0.1875
- temporal_qkv: bfloat16 [1152, 3456], P('space'), may hold values from -0.1875 to 0.1875
- temporal_out: bfloat16 [1152, 1152], P('space'), may hold values from -0.1875 to 0.1875
Outputs:
- latent_grad: bfloat16 [2, 32, 896, 1152], P(None, 'tm', 'space')
The draws below stay inside these ranges and needn't reach their ends.
All inputs are finite; a program needn't handle non-finite values.
Results may differ from the reference program's by a relative error of at most 0.019.
Values may be sent and summed in bfloat16 or wider, within the bound.
No kernel may reach another device: no remote copies, remote signals or barrier semaphores. Data moves between devices by JAX's collectives and lax.ppermute only.
A program may use at most 128 MiB of HBM per device.

```python
import jax
import jax.numpy as jnp
from jax import lax

D = 1152
HD = 72
BATCH = 2
PATCHES = 896
FRAMES = 32


def steps_of(key, dims, split, low, largest):
    def one(axis_at, blocks):
        heights = jax.random.uniform(jax.random.fold_in(jax.random.fold_in(key, 6), axis_at), (blocks,), jnp.float32, low / len(split), largest / len(split))
        return jnp.repeat(jnp.exp(heights), dims[axis_at] // blocks).reshape((-1,) + (1,) * (len(dims) - axis_at - 1))

    gain = one(*split[0])
    for cut in split[1:]:
        gain = gain * one(*cut)
    return gain


def gaussian(stream_key, shape, scale, limit, cuts=(), held_as=jnp.bfloat16):
    values = jax.random.normal(stream_key, shape, jnp.float32) * scale
    if len(cuts) > 0:
        values = steps_of(stream_key, shape, cuts, -0.22, 0.18) * values
    return jnp.clip(values, min=-limit, max=limit).astype(held_as)


def setup_inputs(seed: int = 0) -> dict:
    keys = jax.random.split(jax.random.key(seed), 8)
    latent = gaussian(keys[0], (BATCH, FRAMES, PATCHES, D), 1.0, 6.0, ((1, 16), (2, 16)))
    upstream = gaussian(keys[1], (BATCH, FRAMES, PATCHES, D), 1.0, 6.0, ((1, 16), (2, 16)))
    modulation = gaussian(keys[2], (BATCH, 6, D), 0.5, 3.0, (), jnp.float32)
    spatial_qkv = gaussian(keys[3], (D, 3 * D), D ** -0.5, 0.1875, ((0, 16),))
    spatial_out = gaussian(keys[4], (D, D), D ** -0.5, 0.1875, ((0, 16),))
    temporal_qkv = gaussian(keys[5], (D, 3 * D), D ** -0.5, 0.1875, ((0, 16),))
    temporal_out = gaussian(keys[6], (D, D), D ** -0.5, 0.1875, ((0, 16),))
    return {"latent": latent, "upstream": upstream, "modulation": modulation, "spatial_qkv": spatial_qkv, "spatial_out": spatial_out, "temporal_qkv": temporal_qkv, "temporal_out": temporal_out}


EPS = 1e-06

def modulate(stream, offset, scaling):
    widened = stream.astype(jnp.float32)
    centre = lax.optimization_barrier(jnp.mean(widened, axis=-1, keepdims=True))
    spread = lax.optimization_barrier(jnp.mean(jnp.square(widened - centre), axis=-1, keepdims=True))
    normed = (widened - centre) * lax.rsqrt(spread + EPS)
    return (normed * (1.0 + scaling) + offset).astype(jnp.bfloat16)

def project_qkv(stream, offset, scaling, w_qkv):
    joined = jnp.dot(modulate(stream, offset, scaling), w_qkv, preferred_element_type=jnp.float32).astype(jnp.bfloat16)
    return joined.reshape(stream.shape[:-1] + (3, stream.shape[-1]))

def residual_out(stream, attended, gating, w_out):
    branch = jnp.dot(attended, w_out, preferred_element_type=jnp.float32)
    return (stream.astype(jnp.float32) + gating * branch).astype(jnp.bfloat16)

def attend(queries, key_rows, values):
    scaling = queries.shape[-1] ** (-0.5)
    scores = jnp.einsum('nqd,nkd->nqk', queries.astype(jnp.float32), key_rows.astype(jnp.float32), precision=lax.Precision.HIGHEST) * scaling
    powers = jnp.exp(scores)
    attn_weights = powers / lax.optimization_barrier(jnp.sum(powers, axis=-1, keepdims=True))
    rounded = lax.optimization_barrier(attn_weights.astype(jnp.bfloat16)).astype(jnp.float32)
    return jnp.einsum('nqk,nkd->nqd', rounded, values.astype(jnp.float32), precision=lax.Precision.HIGHEST).astype(jnp.bfloat16)

def attend_single(triple):
    return attend(triple[0][None], triple[1][None], triple[2][None])[0]

def attend_rows(queries, key_rows, values):
    return lax.map(jax.checkpoint(attend_single), (queries, key_rows, values))

def spatial_mix(triple):
    b, f, p, _, c = triple.shape
    heads_here = c // HD
    arranged = triple.reshape(b, f, p, 3, heads_here, HD).transpose(3, 0, 1, 4, 2, 5).reshape(3, b * f * heads_here, p, HD)
    mixture = attend_rows(arranged[0], arranged[1], arranged[2])
    return mixture.reshape(b, f, heads_here, p, HD).transpose(0, 1, 3, 2, 4).reshape(b, f, p, c)

def temporal_mix(triple):
    b, f, p, _, c = triple.shape
    heads_here = c // HD
    arranged = triple.reshape(b, f, p, 3, heads_here, HD).transpose(3, 0, 2, 4, 1, 5).reshape(3, b * p * heads_here, f, HD)
    mixture = attend(arranged[0], arranged[1], arranged[2])
    return mixture.reshape(b, p, heads_here, f, HD).transpose(0, 3, 1, 2, 4).reshape(b, f, p, c)

def reference(latent, upstream, modulation, spatial_qkv, spatial_out, temporal_qkv, temporal_out):
    mod_table = modulation[:, :, None, None, :]

    def forward(stream):
        triple = project_qkv(stream, mod_table[:, 0], mod_table[:, 1], spatial_qkv)
        hidden = residual_out(stream, spatial_mix(triple), mod_table[:, 2], spatial_out)
        triple = project_qkv(hidden, mod_table[:, 3], mod_table[:, 4], temporal_qkv)
        return residual_out(hidden, temporal_mix(triple), mod_table[:, 5], temporal_out)
    _, pull_back = jax.vjp(forward, latent)
    return pull_back(upstream)[0]
```

```python
import functools

import jax
import jax.numpy as jnp
from jax import lax
from jax.experimental import pallas as pl
from jax.experimental.pallas import tpu as pltpu
from jax.sharding import Mesh, PartitionSpec as P

HD = 72
EPS = 1e-06
D = 1152
GW = 288
GP = 384
T = 224
HP = 56
BIG = 60 * 2**20
BF = jnp.bfloat16
F32 = jnp.float32
LOG2E = 1.4426950408889634
SCALE = HD ** (-0.5)

VM = pl.BlockSpec(memory_space=pltpu.VMEM)
SM = pl.BlockSpec(memory_space=pltpu.SMEM)
HBM = pl.BlockSpec(memory_space=pl.ANY)


def sds(shape, dtype=BF):
    return jax.ShapeDtypeStruct(shape, dtype)


def call(body, outs, n_in_specs, scratch=(), **kw):
    return pl.pallas_call(
        body,
        out_shape=outs,
        in_specs=n_in_specs,
        out_specs=jax.tree.map(lambda _: VM, outs),
        scratch_shapes=list(scratch),
        compiler_params=pltpu.CompilerParams(vmem_limit_bytes=BIG),
        **kw,
    )


def mm(a, b):
    return jnp.dot(a, b, preferred_element_type=F32)


def mm_nt(a, b):
    return lax.dot_general(a, b, (((1,), (1,)), ((), ())), preferred_element_type=F32)


def mm_tn(a, b):
    return lax.dot_general(a, b, (((0,), (0,)), ((), ())), preferred_element_type=F32)


def normed(x):
    centre = jnp.mean(x, axis=-1, keepdims=True)
    shifted = x - centre
    rstd = lax.rsqrt(jnp.mean(jnp.square(shifted), axis=-1, keepdims=True) + EPS)
    return shifted * rstd, rstd


def norm_back(dm, x, scaling):
    hat, rstd = normed(x)
    dn = dm.astype(F32) * (1.0 + scaling)
    mean_dn = jnp.mean(dn, axis=-1, keepdims=True)
    mean_hat = jnp.mean(dn * hat, axis=-1, keepdims=True)
    return (rstd * (dn - mean_dn - hat * mean_hat)).astype(BF)


def rows_of(lats):
    return jnp.concatenate([r[...].astype(F32) for r in lats], axis=0)


def norm_kernel(l0, l1, l2, l3, mod, out):
    hat, _ = normed(rows_of((l0, l1, l2, l3)))
    out[...] = (hat * (1.0 + mod[1:2, :]) + mod[0:1, :]).astype(BF)


def tail_to(t6, j):
    lane = lax.broadcasted_iota(jnp.int32, t6.shape, 1)
    moved = t6 if j == 0 else pltpu.roll(t6, 128 - 32 * j, 1)
    return jnp.where(lane < 32, moved, 0.0)


def spatial_fwd(m0, m1, m2, m3, w0, w1, att, q_ref, k_ref, v_ref, p_ref, acc):
    h = pl.program_id(0)

    @pl.when(h == 0)
    def _():
        acc[...] = jnp.zeros_like(acc)
        for k, m in enumerate((m0, m1, m2, m3)):
            rows = slice(k * T, (k + 1) * T)
            r0 = mm(m[...], w0[...])
            r1 = mm(m[...], w1[:, 128:512])
            t6 = r1[:, 256:384]
            q_ref[rows, 0:256] = r0[:, 0:256].astype(BF)
            q_ref[rows, 256:384] = tail_to(t6, 0).astype(BF)
            k_ref[rows, 0:256] = r0[:, 256:512].astype(BF)
            k_ref[rows, 256:384] = tail_to(t6, 1).astype(BF)
            v_ref[rows, 0:256] = r1[:, 0:256].astype(BF)
            v_ref[rows, 256:384] = tail_to(t6, 2).astype(BF)

    start = pl.multiple_of((h // 2) * 128, 128)
    win = pl.ds(start, 256)
    first = HD * h - start
    lane = lax.broadcasted_iota(jnp.int32, (1, 256), 1)
    keep = (lane >= first) & (lane < first + HD)
    kwin = k_ref[:, win]
    vwin = jnp.where(keep, v_ref[:, win], 0)
    for i in range(4):
        rows = slice(i * T, (i + 1) * T)
        qi = jnp.where(keep, q_ref[rows, win], 0)
        s = mm_nt(qi, kwin) * (SCALE * LOG2E)
        e = jnp.exp2(s - jnp.max(s, axis=1, keepdims=True))
        p = (e * (1.0 / jnp.sum(e, axis=1, keepdims=True))).astype(BF)
        p_ref[0, rows, :] = p
        acc[rows, win] += mm(p, vwin)

    @pl.when(h == 3)
    def _():
        for k in range(4):
            att[k] = acc[k * T : (k + 1) * T, :].astype(BF)


def spatial_bwd(d0, d1, d2, d3, q_ref, k_ref, v_ref, p_ref, w0, w1, out, dq, dk, dv):
    h = pl.program_id(0)

    @pl.when(h == 0)
    def _():
        dq[...] = jnp.zeros_like(dq)
        dk[...] = jnp.zeros_like(dk)
        dv[...] = jnp.zeros_like(dv)

    start = pl.multiple_of((h // 2) * 128, 128)
    win = pl.ds(start, 256)
    first = HD * h - start
    lane = lax.broadcasted_iota(jnp.int32, (1, 256), 1)
    keep = (lane >= first) & (lane < first + HD)
    vwin = v_ref[:, win]
    kwin = jnp.where(keep, k_ref[:, win], 0)
    for i, d in enumerate((d0, d1, d2, d3)):
        rows = slice(i * T, (i + 1) * T)
        di = jnp.where(keep, d[:, win], 0)
        qi = jnp.where(keep, q_ref[rows, win], 0)
        pb = p_ref[0, rows, :]
        p = pb.astype(F32)
        dp = mm_nt(di, vwin)
        delta = jnp.sum(dp * p, axis=1, keepdims=True)
        ds = (p * ((dp - delta) * SCALE)).astype(BF)
        dq[rows, win] += mm(ds, kwin)
        dk[:, win] += mm_tn(ds, qi)
        dv[:, win] += mm_tn(pb, di)

    @pl.when(h == 3)
    def _():
        for k in range(4):
            rows = slice(k * T, (k + 1) * T)
            tail = (
                dq[rows, 256:384]
                + pltpu.roll(dk[rows, 256:384], 32, 1)
                + pltpu.roll(dv[rows, 256:384], 64, 1)
            )
            a = jnp.concatenate([dq[rows, 0:256], dk[rows, 0:256]], axis=1).astype(BF)
            b = jnp.concatenate([dv[rows, 0:256], tail], axis=1).astype(BF)
            out[k] = (mm_nt(a, w0[...]) + mm_nt(b, w1[:, 128:512])).astype(BF)


def fetch(src, row0, nrows, col0, ncols, dst, sem):
    return pltpu.make_async_copy(src.at[pl.ds(row0, nrows), pl.ds(col0, ncols)], dst, sem)


def hidden_kernel(pos, a0, a1, a2, a3, l0, l1, l2, l3, mod, wg, out, w, sem):
    copy = fetch(wg, D, D, 1792, D, w, sem)
    copy.start()
    x, y = pos[2], pos[3]
    out[7] = jnp.zeros((4, 8, D), BF)
    copy.wait()
    branch = jnp.zeros((T, D), F32)
    for k, a in enumerate((a0, a1, a2, a3)):
        g = lax.rem(y + k, 4)
        branch += mm(a[:, 0:GW], w[pl.ds(pl.multiple_of(g * GW, 32), GW), :])
    hidden = rows_of((l0, l1, l2, l3)) + mod[2:3, :] * branch
    for k in range(4):
        xs = lax.rem(x + 4 - k, 4)
        for j in range(7):
            r = k * HP + 8 * j
            out[j, xs] = hidden[r : r + 8, :].astype(BF)


def temporal_kernel(hid, up, mod, wg, out, w0, w1, qkv, dout, dqkv, sems):
    first = fetch(wg, 0, D, 0, 2944, w0, sems.at[0])
    second = fetch(wg, D, D, 128, 1664, w1, sems.at[1])
    first.start()
    second.start()
    n = hid.shape[0]
    x = hid[...].astype(F32)
    hat, _ = normed(x)
    m = (hat * (1.0 + mod[4:5, :]) + mod[3:4, :]).astype(BF)
    g = (up[...].astype(F32) * mod[5:6, :]).astype(BF)
    first.wait()
    qkv[:, 0:2944] = mm(m, w0[...]).astype(BF)
    second.wait()
    qkv[:, 2944:3456] = mm(m, w1[:, 0:512]).astype(BF)
    dout[...] = mm_nt(g, w1[:, 512:1664]).astype(BF)
    dqkv[...] = jnp.zeros_like(dqkv)
    ri = lax.broadcasted_iota(jnp.int32, (n, n), 0)
    ci = lax.broadcasted_iota(jnp.int32, (n, n), 1)
    same = (ri & 7) == (ci & 7)
    lane = lax.broadcasted_iota(jnp.int32, (1, 256), 1)
    for h in range(16):
        start = min(128 * (HD * h // 128), D - 256)
        first_lane = HD * h - start
        keep = (lane >= first_lane) & (lane < first_lane + HD)
        qw = slice(start, start + 256)
        kw = slice(D + start, D + start + 256)
        vw = slice(2 * D + start, 2 * D + start + 256)
        q = jnp.where(keep, qkv[:, qw], 0)
        k = jnp.where(keep, qkv[:, kw], 0)
        v = qkv[:, vw]
        d = jnp.where(keep, dout[:, qw], 0)
        s = jnp.where(same, mm_nt(q, k) * (SCALE * LOG2E), -1e30)
        e = jnp.exp2(s - jnp.max(s, axis=1, keepdims=True))
        e = jnp.where(same, e, 0.0)
        p = e * (1.0 / jnp.sum(e, axis=1, keepdims=True))
        pb = p.astype(BF)
        dp = mm_nt(d, v)
        delta = jnp.sum(dp * p, axis=1, keepdims=True)
        ds = (p * ((dp - delta) * SCALE)).astype(BF)
        dqkv[:, qw] += mm(ds, k)
        dqkv[:, kw] += mm_tn(ds, q)
        dqkv[:, vw] += mm_tn(pb, d)
    dm = mm_nt(dqkv[:, 0:2944].astype(BF), w0[...])
    dm += mm_nt(dqkv[:, 2944:3456].astype(BF), w1[:, 0:512])
    through = norm_back(dm.astype(BF), x, mod[4:5, :])
    out[...] = (up[...].astype(F32) + through.astype(F32)).astype(BF)


def attended_back(pos, back, mod, wg, grad, datt, w, sem):
    copy = fetch(wg, D, D, 1792, D, w, sem)
    copy.start()
    x, y = pos[2], pos[3]
    pieces = []
    for k in range(4):
        xs = lax.rem(x + 4 - k, 4)
        for j in range(7):
            pieces.append(back[j, xs].astype(F32))
    gh = jnp.concatenate(pieces, axis=0)
    grad[...] = gh.astype(BF)
    g = (gh * mod[2:3, :]).astype(BF)
    copy.wait()
    for k in range(4):
        grp = lax.rem(y + k, 4)
        r = mm_nt(g, w[pl.ds(pl.multiple_of(grp * GW, 32), GW), :])
        datt[k] = jnp.concatenate([r, jnp.zeros((T, GP - GW), F32)], axis=1).astype(BF)


def close_kernel(s0, s1, s2, s3, l0, l1, l2, l3, gh, mod, out):
    dm = s0[...].astype(F32) + s1[...].astype(F32) + s2[...].astype(F32) + s3[...].astype(F32)
    through = norm_back(dm.astype(BF), rows_of((l0, l1, l2, l3)), mod[1:2, :])
    total = gh[...].astype(F32) + through.astype(F32)
    for k in range(4):
        out[k] = total[k * HP : (k + 1) * HP, :].astype(BF)


def move(x, axis, n, k):
    if k % n == 0:
        return x
    return lax.ppermute(x, axis, [(i, (i + k) % n) for i in range(n)])


def pick(x, i):
    return lax.dynamic_index_in_dim(x, i, 0, keepdims=False)


def shards(latent, upstream, modulation, spatial_qkv, spatial_out, temporal_qkv, temporal_out):
    z, c, x, y = (lax.axis_index(a) for a in ("z", "c", "x", "y"))
    pos = jnp.stack([z, c, x, y]).astype(jnp.int32)
    mod = pick(modulation, c)

    wide = jnp.concatenate([temporal_qkv, temporal_out, spatial_out], axis=1)
    wide = lax.dynamic_slice_in_dim(wide, c * 2816, 2944, axis=1)
    wg = lax.all_gather(wide, ("c", "x", "y"), axis=0, tiled=True)

    def to_sample(t):
        own = pick(t, c)
        return jnp.concatenate([own, move(pick(t, 1 - c), "c", 2, 1)], axis=0)

    lat4 = to_sample(latent)
    lats = [move(pick(lat4, lax.rem(x + k, 4)), "x", 4, k) for k in range(4)]

    parts = spatial_qkv.reshape(72, 3, 4, GW)
    dense = jnp.concatenate(
        [parts[:, j, :, 0:256] for j in range(3)]
        + [parts[:, j, :, 256:GW] for j in range(3)]
        + [jnp.zeros((72, 4, 32), BF)],
        axis=-1,
    )
    dense = lax.dynamic_slice_in_dim(dense, c * 384, 512, axis=2).transpose(1, 0, 2)
    send = jnp.concatenate([dense] * 4, axis=0)
    wh = lax.all_to_all(send, ("x", "y"), split_axis=0, concat_axis=0, tiled=True)
    wh = wh.reshape(D, 512)
    wo = move(wh, "c", 2, 1)
    ws0 = jnp.where(c == 0, wh, wo)
    ws1 = jnp.where(c == 0, wo, wh)

    m = call(norm_kernel, sds((T, D)), [VM] * 5)(*lats, mod)
    ms = [move(m, "y", 4, k) for k in range(4)]

    up4 = to_sample(upstream).reshape(4, 7, 8, D).transpose(1, 0, 2, 3)
    up4 = jnp.concatenate([up4, jnp.zeros((1, 4, 8, D), BF)], axis=0)
    up_t = lax.all_to_all(up4, "z", split_axis=0, concat_axis=0, tiled=True).reshape(256, D)

    whole = lambda *shape: pl.BlockSpec(shape, lambda h: (0,) * len(shape))
    pspec = pl.BlockSpec((1, 896, 896), lambda h: (h, 0, 0))
    att, q, k, v, probs = pl.pallas_call(
        spatial_fwd,
        grid=(4,),
        in_specs=[whole(T, D)] * 4 + [whole(D, 512)] * 2,
        out_specs=[whole(4, T, GP)] + [whole(896, GP)] * 3 + [pspec],
        out_shape=[sds((4, T, GP))] + [sds((896, GP))] * 3 + [sds((4, 896, 896))],
        scratch_shapes=[pltpu.VMEM((896, GP), F32)],
        compiler_params=pltpu.CompilerParams(vmem_limit_bytes=BIG),
    )(*ms, ws0, ws1)
    atts = [move(att[k_], "y", 4, -k_) for k_ in range(4)]

    wscr = [pltpu.VMEM((D, D), BF), pltpu.SemaphoreType.DMA]
    hid = call(hidden_kernel, sds((8, 4, 8, D)), [SM] + [VM] * 9 + [HBM], wscr)(
        pos, *atts, *lats, mod, wg
    )
    hid_t = lax.all_to_all(
        hid.reshape(32, 8, D), ("z", "x"), split_axis=0, concat_axis=0, tiled=True
    ).reshape(256, D)

    grad_t = call(
        temporal_kernel,
        sds((256, D)),
        [VM] * 3 + [HBM],
        [
            pltpu.VMEM((D, 2944), BF),
            pltpu.VMEM((D, 1664), BF),
            pltpu.VMEM((256, 3 * D), BF),
            pltpu.VMEM((256, D), BF),
            pltpu.VMEM((256, 3 * D), F32),
            pltpu.SemaphoreType.DMA((2,)),
        ],
    )(hid_t, up_t, mod, wg)

    back = lax.all_to_all(
        grad_t.reshape(32, 8, D), ("z", "x"), split_axis=0, concat_axis=0, tiled=True
    ).reshape(8, 4, 8, D)
    gh, datt = call(
        attended_back, (sds((T, D)), sds((4, T, GP))), [SM, VM, VM, HBM], wscr
    )(pos, back, mod, wg)
    datts = [move(datt[k_], "y", 4, k_) for k_ in range(4)]

    partial = pl.pallas_call(
        spatial_bwd,
        grid=(4,),
        in_specs=[whole(T, GP)] * 4 + [whole(896, GP)] * 3 + [pspec] + [whole(D, 512)] * 2,
        out_specs=whole(4, T, D),
        out_shape=sds((4, T, D)),
        scratch_shapes=[pltpu.VMEM((896, GP), F32)] * 3,
        compiler_params=pltpu.CompilerParams(vmem_limit_bytes=BIG),
    )(*datts, q, k, v, probs, ws0, ws1)
    sums = [move(partial[k_], "y", 4, -k_) for k_ in range(4)]

    lg = call(close_kernel, sds((4, HP, D)), [VM] * 10)(*sums, *lats, gh, mod)
    got = jnp.stack([move(lg[k_], "x", 4, -k_) for k_ in range(4)])
    frames = [pick(got, lax.rem(f - x + 4, 4)) for f in range(4)]
    own = jnp.stack(frames[0:2])
    other = move(jnp.stack(frames[2:4]), "c", 2, 1)
    return jnp.where(c == 0, jnp.stack([own, other]), jnp.stack([other, own]))


def solution(mesh):
    split = Mesh(mesh.devices.reshape(8, 2, 4, 4), ("z", "c", "x", "y"))
    tokens = P(None, ("z", "c"), ("x", "y"), None)
    rows = P(("x", "y"), None)
    return jax.shard_map(
        shards,
        mesh=split,
        in_specs=(tokens, tokens, P(), rows, rows, rows, rows),
        out_specs=tokens,
        check_vma=False,
    )
```

```python
import jax
import jax.numpy as jnp
from jax import lax
from jax.experimental import pallas as pl
from jax.experimental.pallas import tpu as pltpu
from jax.sharding import Mesh, PartitionSpec as P

HD = 72
EPS = 1e-06
D = 1152
GW = 288
GP = 384
T = 224
ROWS = 88
HP = 56
BIG = 60 * 2**20
BF = jnp.bfloat16
F32 = jnp.float32
LOG2E = 1.4426950408889634
SCALE = HD ** (-0.5)

VM = pl.BlockSpec(memory_space=pltpu.VMEM)
SM = pl.BlockSpec(memory_space=pltpu.SMEM)
HBM = pl.BlockSpec(memory_space=pl.ANY)


def sds(shape, dtype=BF):
    return jax.ShapeDtypeStruct(shape, dtype)


def call(body, outs, n_in_specs, scratch=(), **kw):
    return pl.pallas_call(
        body,
        out_shape=outs,
        in_specs=n_in_specs,
        out_specs=jax.tree.map(lambda _: VM, outs),
        scratch_shapes=list(scratch),
        compiler_params=pltpu.CompilerParams(vmem_limit_bytes=BIG),
        **kw,
    )


def mm(a, b):
    return jnp.dot(a, b, preferred_element_type=F32)


def mm_nt(a, b):
    return lax.dot_general(a, b, (((1,), (1,)), ((), ())), preferred_element_type=F32)


def mm_tn(a, b):
    return lax.dot_general(a, b, (((0,), (0,)), ((), ())), preferred_element_type=F32)


def normed(x):
    centre = jnp.mean(x, axis=-1, keepdims=True)
    shifted = x - centre
    rstd = lax.rsqrt(jnp.mean(jnp.square(shifted), axis=-1, keepdims=True) + EPS)
    return shifted * rstd, rstd


def norm_back(dm, x, scaling):
    hat, rstd = normed(x)
    dn = dm.astype(F32) * (1.0 + scaling)
    mean_dn = jnp.mean(dn, axis=-1, keepdims=True)
    mean_hat = jnp.mean(dn * hat, axis=-1, keepdims=True)
    return (rstd * (dn - mean_dn - hat * mean_hat)).astype(BF)


def rows_of(lats):
    return jnp.concatenate([r[...].astype(F32) for r in lats], axis=0)


def first_kernel(pos, own, other, mod, w, out):
    wide = w[...].astype(F32)
    first = pos[1] == 0
    for g in range(4):
        q, k, v = (wide[:, j * D + g * GW : j * D + (g + 1) * GW] for j in range(3))
        low = jnp.concatenate([q[:, 0:256], k[:, 0:256]], axis=1)
        tail = jnp.concatenate(
            [q[:, 256:GW], k[:, 256:GW], v[:, 256:GW], jnp.zeros((HD, 32), F32)], axis=1
        )
        high = jnp.concatenate([k[:, 128:256], v[:, 0:256], tail], axis=1)
        half = jnp.where(first, low, high)
        lines = [
            jnp.concatenate(
                [half[8 * r : 8 * r + 8, 128 * i : 128 * i + 128] for r in range(9)], axis=1
            )
            for i in range(4)
        ]
        lines = jnp.concatenate(lines, axis=0).astype(BF)
        for f in range(4):
            out[4 * f + g, HP:ROWS, :] = lines
    for f in range(4):
        src = own if f < 2 else other
        hat, _ = normed(src[f % 2].astype(F32))
        m = (hat * (1.0 + mod[1:2, :]) + mod[0:1, :]).astype(BF)
        for g in range(4):
            out[4 * f + g, 0:HP, :] = m


def sort_kernel(pos, l0, l1, u0, u1, out):
    out[lax.rem(15 - pos[0], 8)] = jnp.zeros((4, 2, 8, D), BF)
    for i, (own, other) in enumerate(((l0, l1), (u0, u1))):
        for f in range(4):
            v = (own if f < 2 else other)[f % 2].astype(F32)
            for j in range(7):
                out[lax.rem(8 + j - pos[0], 8), f, i] = v[8 * j : 8 * j + 8, :].astype(BF)


def tail_to(t6, j):
    lane = lax.broadcasted_iota(jnp.int32, t6.shape, 1)
    moved = t6 if j == 0 else pltpu.roll(t6, 128 - 32 * j, 1)
    return jnp.where(lane < 32, moved, 0.0)


def spatial_fwd(pos, m_ref, wb, att, q_ref, k_ref, v_ref, p_ref, ws, acc):
    h = pl.program_id(0)

    @pl.when(h == 0)
    def _():
        acc[...] = jnp.zeros_like(acc)
        for half, src, at in ((pos[1], m_ref, HP), (1 - pos[1], wb, 0)):
            for i in range(4):
                v = src[:, at + 8 * i : at + 8 * i + 8, :].astype(F32)
                v = [v[:, :, 128 * r : 128 * r + 128] for r in range(9)]
                v = jnp.concatenate(v, axis=1).reshape(D, 128)
                ws[half, :, 128 * i : 128 * i + 128] = v.astype(BF)
        for k in range(4):
            rows = slice(k * T, (k + 1) * T)
            m = [m_ref[4 * k + i, 0:HP, :].astype(F32) for i in range(4)]
            m = jnp.concatenate(m, axis=0).astype(BF)
            r0 = mm(m, ws[0])
            r1 = mm(m, ws[1, :, 128:512])
            t6 = r1[:, 256:384]
            q_ref[rows, 0:256] = r0[:, 0:256].astype(BF)
            q_ref[rows, 256:384] = tail_to(t6, 0).astype(BF)
            k_ref[rows, 0:256] = r0[:, 256:512].astype(BF)
            k_ref[rows, 256:384] = tail_to(t6, 1).astype(BF)
            v_ref[rows, 0:256] = r1[:, 0:256].astype(BF)
            v_ref[rows, 256:384] = tail_to(t6, 2).astype(BF)

    start = pl.multiple_of((h // 2) * 128, 128)
    win = pl.ds(start, 256)
    first = HD * h - start
    lane = lax.broadcasted_iota(jnp.int32, (1, 256), 1)
    keep = (lane >= first) & (lane < first + HD)
    kwin = k_ref[:, win]
    vwin = jnp.where(keep, v_ref[:, win], 0)
    for i in range(4):
        rows = slice(i * T, (i + 1) * T)
        qi = jnp.where(keep, q_ref[rows, win], 0)
        s = mm_nt(qi, kwin) * (SCALE * LOG2E)
        e = jnp.exp2(s - jnp.max(s, axis=1, keepdims=True))
        p = (e * (1.0 / jnp.sum(e, axis=1, keepdims=True))).astype(BF)
        p_ref[0, rows, :] = p
        acc[rows, win] += mm(p, vwin)

    @pl.when(h == 3)
    def _():
        att[7] = jnp.zeros((16, 8, GP), BF)
        for s in range(16):
            for j in range(7):
                r = s * HP + 8 * j
                att[j, s] = acc[r : r + 8, :].astype(BF)


def spatial_bwd(d_ref, q_ref, k_ref, v_ref, p_ref, ws, out, datt, dq, dk, dv):
    h = pl.program_id(0)

    @pl.when(h == 0)
    def _():
        dq[...] = jnp.zeros_like(dq)
        dk[...] = jnp.zeros_like(dk)
        dv[...] = jnp.zeros_like(dv)
        for s in range(16):
            for j in range(7):
                r = s * HP + 8 * j
                datt[r : r + 8, :] = d_ref[j, s].astype(F32)

    start = pl.multiple_of((h // 2) * 128, 128)
    win = pl.ds(start, 256)
    first = HD * h - start
    lane = lax.broadcasted_iota(jnp.int32, (1, 256), 1)
    keep = (lane >= first) & (lane < first + HD)
    vwin = v_ref[:, win]
    kwin = jnp.where(keep, k_ref[:, win], 0)
    for i in range(4):
        rows = slice(i * T, (i + 1) * T)
        di = jnp.where(keep, datt[rows, win], 0.0).astype(BF)
        qi = jnp.where(keep, q_ref[rows, win], 0)
        pb = p_ref[0, rows, :]
        p = pb.astype(F32)
        dp = mm_nt(di, vwin)
        delta = jnp.sum(dp * p, axis=1, keepdims=True)
        ds = (p * ((dp - delta) * SCALE)).astype(BF)
        dq[rows, win] += mm(ds, kwin)
        dk[:, win] += mm_tn(ds, qi)
        dv[:, win] += mm_tn(pb, di)

    @pl.when(h == 3)
    def _():
        for k in range(4):
            rows = slice(k * T, (k + 1) * T)
            tail = (
                dq[rows, 256:384]
                + pltpu.roll(dk[rows, 256:384], 32, 1)
                + pltpu.roll(dv[rows, 256:384], 64, 1)
            )
            a = jnp.concatenate([dq[rows, 0:256], dk[rows, 0:256]], axis=1).astype(BF)
            b = jnp.concatenate([dv[rows, 0:256], tail], axis=1).astype(BF)
            out[rows, :] = (mm_nt(a, ws[0]) + mm_nt(b, ws[1, :, 128:512])).astype(BF)


def rows64(v):
    return v.astype(F32).reshape(64, v.shape[-1])


def temporal_kernel(pos, att, *refs):
    lus, (mod, wg, grad, datt, w0, w1, lu, qkv, dout, dqkv, sems) = refs[:8], refs[8:]
    second = pltpu.make_async_copy(wg.at[pl.ds(D, D), pl.ds(128, 2816)], w1, sems.at[1])
    first = pltpu.make_async_copy(wg.at[pl.ds(0, D), :], w0, sems.at[0])
    second.start()
    first.start()
    n = 256
    for k in range(8):
        lu[lax.rem(pos[0] + 8 - k, 8)] = lus[k][...]
    lat = jnp.concatenate([rows64(lu[:, f, 0]) for f in range(4)], axis=0)
    up = jnp.concatenate([rows64(lu[:, f, 1]) for f in range(4)], axis=0)
    second.wait()
    branch = jnp.zeros((n, D), F32)
    for g in range(4):
        a = jnp.concatenate([rows64(att[:, 4 * f + g]) for f in range(4)], axis=0).astype(BF)
        branch += mm(a[:, 0:GW], w1[g * GW : (g + 1) * GW, 1664:2816])
    x = (lat + mod[2:3, :] * branch).astype(BF).astype(F32)
    hat, _ = normed(x)
    m = (hat * (1.0 + mod[4:5, :]) + mod[3:4, :]).astype(BF)
    gated = (up * mod[5:6, :]).astype(BF)
    dout[...] = mm_nt(gated, w1[:, 512:1664]).astype(BF)
    qkv[:, 2944:3456] = mm(m, w1[:, 0:512]).astype(BF)
    first.wait()
    qkv[:, 0:2944] = mm(m, w0[...]).astype(BF)
    dqkv[...] = jnp.zeros_like(dqkv)
    ri = lax.broadcasted_iota(jnp.int32, (n, n), 0)
    ci = lax.broadcasted_iota(jnp.int32, (n, n), 1)
    same = (ri & 7) == (ci & 7)
    lane = lax.broadcasted_iota(jnp.int32, (1, 256), 1)
    for h in range(16):
        start = min(128 * (HD * h // 128), D - 256)
        first_lane = HD * h - start
        keep = (lane >= first_lane) & (lane < first_lane + HD)
        qw = slice(start, start + 256)
        kw = slice(D + start, D + start + 256)
        vw = slice(2 * D + start, 2 * D + start + 256)
        q = jnp.where(keep, qkv[:, qw], 0)
        k = jnp.where(keep, qkv[:, kw], 0)
        v = qkv[:, vw]
        d = jnp.where(keep, dout[:, qw], 0)
        s = jnp.where(same, mm_nt(q, k) * (SCALE * LOG2E), -1e30)
        e = jnp.exp2(s - jnp.max(s, axis=1, keepdims=True))
        e = jnp.where(same, e, 0.0)
        p = e * (1.0 / jnp.sum(e, axis=1, keepdims=True))
        pb = p.astype(BF)
        dp = mm_nt(d, v)
        delta = jnp.sum(dp * p, axis=1, keepdims=True)
        ds = (p * ((dp - delta) * SCALE)).astype(BF)
        dqkv[:, qw] += mm(ds, k)
        dqkv[:, kw] += mm_tn(ds, q)
        dqkv[:, vw] += mm_tn(pb, d)
    dm = mm_nt(dqkv[:, 0:2944].astype(BF), w0[...])
    dm += mm_nt(dqkv[:, 2944:3456].astype(BF), w1[:, 0:512])
    through = norm_back(dm.astype(BF), x, mod[4:5, :])
    gh = (up + through.astype(F32)).astype(BF).astype(F32)
    for f in range(4):
        grad[:, f] = gh[64 * f : 64 * f + 64, :].reshape(8, 8, D).astype(BF)
    gated = (gh * mod[2:3, :]).astype(BF)
    for g in range(4):
        r = mm_nt(gated, w1[g * GW : (g + 1) * GW, 1664:2816])
        r = jnp.concatenate([r, jnp.zeros((n, GP - GW), F32)], axis=1)
        for f in range(4):
            datt[:, 4 * f + g] = r[64 * f : 64 * f + 64, :].reshape(8, 8, GP).astype(BF)


def close_kernel(dm_ref, l0, l1, gh, mod, own, other):
    for f in range(4):
        dm = sum(dm_ref[4 * f + g].astype(F32) for g in range(4))
        src = (l0 if f < 2 else l1)[f % 2].astype(F32)
        through = norm_back(dm.astype(BF), src, mod[1:2, :])
        g = jnp.concatenate([gh[j, f].astype(F32) for j in range(7)], axis=0)
        (own if f < 2 else other)[f % 2] = (g + through.astype(F32)).astype(BF)


def pick(v, i):
    return lax.dynamic_index_in_dim(v, i, 0, keepdims=False)


def move(v, axis, n, k):
    if k % n == 0:
        return v
    return lax.ppermute(v, axis, [(i, (i + k) % n) for i in range(n)])


def a2a(v, axes):
    return lax.all_to_all(v, axes, split_axis=0, concat_axis=0, tiled=True)


def after(v, *others):
    return lax.optimization_barrier((v,) + others)[0]


def shards(latent, upstream, modulation, spatial_qkv, spatial_out, temporal_qkv, temporal_out):
    z, c, x, y = (lax.axis_index(a) for a in ("z", "c", "x", "y"))
    pos = jnp.stack([z, c, x, y]).astype(jnp.int32)
    mod = pick(modulation, c)
    swap = lambda v: lax.ppermute(v, "c", [(0, 1), (1, 0)])
    space = ("x", "y")

    l_own = pick(latent, c)
    l_other = swap(pick(latent, 1 - c))

    wide = jnp.concatenate([temporal_qkv, temporal_out, spatial_out], axis=1)
    wide = lax.dynamic_slice_in_dim(wide, c * 2816, 2944, axis=1)
    wg = lax.all_gather(wide, ("c", "x", "y"), axis=0, tiled=True)

    first = call(first_kernel, sds((16, ROWS, D)), [SM] + [VM] * 4)(
        pos, l_own, l_other, mod, spatial_qkv
    )
    got = a2a(first, space)

    up = after(upstream, first)
    sorted_ = call(sort_kernel, sds((8, 4, 2, 8, D)), [SM] + [VM] * 4)(
        pos, l_own, l_other, pick(up, c), swap(pick(up, 1 - c))
    )
    lus = [move(sorted_[k], "z", 8, k) for k in range(8)]
    got = after(got, *lus)
    wb = swap(got[:, HP:ROWS, :])

    whole = lambda *shape: pl.BlockSpec(shape, lambda h: (0,) * len(shape))
    pspec = pl.BlockSpec((1, 896, 896), lambda h: (h, 0, 0))
    att, q, k, v, probs, ws = pl.pallas_call(
        spatial_fwd,
        grid=(4,),
        in_specs=[SM, whole(16, ROWS, D), whole(16, 32, D)],
        out_specs=[whole(8, 16, 8, GP)] + [whole(896, GP)] * 3 + [pspec, whole(2, D, 512)],
        out_shape=[sds((8, 16, 8, GP))]
        + [sds((896, GP))] * 3
        + [sds((4, 896, 896)), sds((2, D, 512))],
        scratch_shapes=[pltpu.VMEM((896, GP), F32)],
        compiler_params=pltpu.CompilerParams(vmem_limit_bytes=BIG),
    )(pos, got, wb)
    att_t = a2a(att.reshape(128, 8, GP), ("z", "x", "y")).reshape(8, 16, 8, GP)

    grad_t, datt = call(
        temporal_kernel,
        (sds((8, 4, 8, D)), sds((8, 16, 8, GP))),
        [SM] + [VM] * 10 + [HBM],
        [
            pltpu.VMEM((D, 2944), BF),
            pltpu.VMEM((D, 2816), BF),
            pltpu.VMEM((8, 4, 2, 8, D), BF),
            pltpu.VMEM((256, 3 * D), BF),
            pltpu.VMEM((256, D), BF),
            pltpu.VMEM((256, 3 * D), F32),
            pltpu.SemaphoreType.DMA((2,)),
        ],
    )(pos, att_t, *lus, mod, wg)

    datt_s = a2a(datt.reshape(128, 8, GP), ("z", "x", "y")).reshape(8, 16, 8, GP)
    gh = a2a(after(grad_t, datt_s), "z")

    partial = pl.pallas_call(
        spatial_bwd,
        grid=(4,),
        in_specs=[whole(8, 16, 8, GP)] + [whole(896, GP)] * 3 + [pspec, whole(2, D, 512)],
        out_specs=whole(896, D),
        out_shape=sds((896, D)),
        scratch_shapes=[pltpu.VMEM((896, GP), F32)] * 4,
        compiler_params=pltpu.CompilerParams(vmem_limit_bytes=BIG),
    )(datt_s, q, k, v, probs, ws)
    dm = a2a(partial.reshape(16, HP, D), space)

    own, other = call(close_kernel, (sds((2, HP, D)),) * 2, [VM] * 5)(
        dm, l_own, l_other, gh, mod
    )
    other = swap(other)
    return jnp.where(c == 0, jnp.stack([own, other]), jnp.stack([other, own]))


def solution(mesh):
    split = Mesh(mesh.devices.reshape(8, 2, 4, 4), ("z", "c", "x", "y"))
    tokens = P(None, ("z", "c"), ("x", "y"), None)
    rows = P(("x", "y"), None)
    return jax.shard_map(
        shards,
        mesh=split,
        in_specs=(tokens, tokens, P(), rows, rows, rows, rows),
        out_specs=tokens,
        check_vma=False,
    )
```

```python
import jax
import jax.numpy as jnp
import ml_dtypes
import numpy as np
from jax import lax
from jax.experimental import pallas as pl
from jax.experimental.pallas import tpu as pltpu
from jax.sharding import Mesh, PartitionSpec as P

HD = 72
EPS = 1e-06
D = 1152
GW = 288
GP = 384
T = 224
ROWS = 88
HP = 56
BIG = 60 * 2**20
BF = jnp.bfloat16
F32 = jnp.float32
LOG2E = 1.4426950408889634
SCALE = HD ** (-0.5)

def _tables():
    row7, row8, lane = np.arange(T), np.arange(256), np.arange(256)
    spread7 = (row8[:, None] // 8 == row7[None] // 7) & (row8[:, None] % 8 == row7[None] % 7)
    collect7 = (row8[:, None] // 8 == row7[None] // 7) & (row8[:, None] % 8 == 7)
    collect8 = (row8[:, None] // 8 == row8[None] // 8) & (row8[:, None] % 8 == 7)
    keep7 = row7[:, None] % 7 == lane[None] // 32
    keep8 = (row8[:, None] % 8 == lane[None] // 32) & (row8[:, None] % 8 < 7)
    body8 = np.broadcast_to(row8[:, None] % 8 < 7, (256, 256))
    fold = np.stack([lane[:, None] % 32 + 32 * g == np.arange(128)[None] for g in range(4)])
    to8 = np.concatenate([spread7, collect7], axis=1)
    return tuple(
        np.asarray(t, dtype=ml_dtypes.bfloat16)
        for t in (to8, to8.T, collect8, collect8.T, keep7, keep8, body8, fold)
    )


TO8, FROM8, COLLECT, SHARE, KEEP7, KEEP8, BODY, FOLD = _tables()

VM = pl.BlockSpec(memory_space=pltpu.VMEM)
SM = pl.BlockSpec(memory_space=pltpu.SMEM)
HBM = pl.BlockSpec(memory_space=pl.ANY)


def sds(shape, dtype=BF):
    return jax.ShapeDtypeStruct(shape, dtype)


def call(body, outs, n_in_specs, scratch=(), **kw):
    return pl.pallas_call(
        body,
        out_shape=outs,
        in_specs=n_in_specs,
        out_specs=jax.tree.map(lambda _: VM, outs),
        scratch_shapes=list(scratch),
        compiler_params=pltpu.CompilerParams(vmem_limit_bytes=BIG),
        **kw,
    )


def mm(a, b):
    return jnp.dot(a, b, preferred_element_type=F32)


def mm_nt(a, b):
    return lax.dot_general(a, b, (((1,), (1,)), ((), ())), preferred_element_type=F32)


def mm_tn(a, b):
    return lax.dot_general(a, b, (((0,), (0,)), ((), ())), preferred_element_type=F32)


def normed(x):
    centre = jnp.mean(x, axis=-1, keepdims=True)
    shifted = x - centre
    rstd = lax.rsqrt(jnp.mean(jnp.square(shifted), axis=-1, keepdims=True) + EPS)
    return shifted * rstd, rstd


def norm_back(dm, x, scaling):
    hat, rstd = normed(x)
    dn = dm.astype(F32) * (1.0 + scaling)
    mean_dn = jnp.mean(dn, axis=-1, keepdims=True)
    mean_hat = jnp.mean(dn * hat, axis=-1, keepdims=True)
    return (rstd * (dn - mean_dn - hat * mean_hat)).astype(BF)


def rows_of(lats):
    return jnp.concatenate([r[...].astype(F32) for r in lats], axis=0)


def first_kernel(pos, own, other, mod, w, out):
    wide = w[...].astype(F32)
    first = pos[1] == 0
    for g in range(4):
        q, k, v = (wide[:, j * D + g * GW : j * D + (g + 1) * GW] for j in range(3))
        low = jnp.concatenate([q[:, 0:256], k[:, 0:256]], axis=1)
        tail = jnp.concatenate(
            [q[:, 256:GW], k[:, 256:GW], v[:, 256:GW], jnp.zeros((HD, 32), F32)], axis=1
        )
        high = jnp.concatenate([k[:, 128:256], v[:, 0:256], tail], axis=1)
        half = jnp.where(first, low, high)
        lines = [
            jnp.concatenate(
                [half[8 * r : 8 * r + 8, 128 * i : 128 * i + 128] for r in range(9)], axis=1
            )
            for i in range(4)
        ]
        lines = jnp.concatenate(lines, axis=0).astype(BF)
        for f in range(4):
            out[4 * f + g, HP:ROWS, :] = lines
    for f in range(4):
        src = own if f < 2 else other
        hat, _ = normed(src[f % 2].astype(F32))
        m = (hat * (1.0 + mod[1:2, :]) + mod[0:1, :]).astype(BF)
        for g in range(4):
            out[4 * f + g, 0:HP, :] = m


def sort_kernel(pos, l0, l1, u0, u1, to8, out):
    for i, pair in enumerate(((l0, l1), (u0, u1))):
        v = [src[f].astype(F32) for src in pair for f in range(2)]
        v = jnp.concatenate(v, axis=0).astype(BF)
        v = mm(to8[:, 0:T], v).astype(BF).astype(F32)
        for f in range(4):
            for j in range(8):
                r = 64 * f + 8 * j
                out[lax.rem(8 + j - pos[0], 8), f, i] = v[r : r + 8, :].astype(BF)


def tail_to(t6, j):
    lane = lax.broadcasted_iota(jnp.int32, t6.shape, 1)
    moved = t6 if j == 0 else pltpu.roll(t6, 128 - 32 * j, 1)
    return jnp.where(lane < 32, moved, 0.0)


def spatial_fwd(pos, m_ref, wb, to8, keep7, att, q_ref, k_ref, v_ref, p_ref, ws, acc):
    h = pl.program_id(0)

    @pl.when(h == 0)
    def _():
        acc[...] = jnp.zeros_like(acc)
        for half, src, at in ((pos[1], m_ref, HP), (1 - pos[1], wb, 0)):
            for i in range(4):
                v = src[:, at + 8 * i : at + 8 * i + 8, :].astype(F32)
                v = [v[:, :, 128 * r : 128 * r + 128] for r in range(9)]
                v = jnp.concatenate(v, axis=1).reshape(D, 128)
                ws[half, :, 128 * i : 128 * i + 128] = v.astype(BF)
        for k in range(4):
            rows = slice(k * T, (k + 1) * T)
            m = [m_ref[4 * k + i, 0:HP, :].astype(F32) for i in range(4)]
            m = jnp.concatenate(m, axis=0).astype(BF)
            r0 = mm(m, ws[0])
            r1 = mm(m, ws[1, :, 128:512])
            t6 = r1[:, 256:384]
            q_ref[rows, 0:256] = r0[:, 0:256].astype(BF)
            q_ref[rows, 256:384] = tail_to(t6, 0).astype(BF)
            k_ref[rows, 0:256] = r0[:, 256:512].astype(BF)
            k_ref[rows, 256:384] = tail_to(t6, 1).astype(BF)
            v_ref[rows, 0:256] = r1[:, 0:256].astype(BF)
            v_ref[rows, 256:384] = tail_to(t6, 2).astype(BF)

    start = pl.multiple_of((h // 2) * 128, 128)
    win = pl.ds(start, 256)
    first = HD * h - start
    lane = lax.broadcasted_iota(jnp.int32, (1, 256), 1)
    keep = (lane >= first) & (lane < first + HD)
    kwin = k_ref[:, win]
    vwin = jnp.where(keep, v_ref[:, win], 0)
    for i in range(4):
        rows = slice(i * T, (i + 1) * T)
        qi = jnp.where(keep, q_ref[rows, win], 0)
        s = mm_nt(qi, kwin) * (SCALE * LOG2E)
        e = jnp.exp2(s - jnp.max(s, axis=1, keepdims=True))
        p = (e * (1.0 / jnp.sum(e, axis=1, keepdims=True))).astype(BF)
        p_ref[0, rows, :] = p
        acc[rows, win] += mm(p, vwin)

    @pl.when(h == 3)
    def _():
        for k in range(4):
            rows = slice(k * T, (k + 1) * T)
            tail = acc[rows, 256:384]
            tail = tail + pltpu.roll(tail, 32, 1)
            tail = tail + pltpu.roll(tail, 64, 1)
            tail = jnp.concatenate([tail, tail], axis=1).astype(BF) * keep7[...]
            v = jnp.concatenate([acc[rows, 0:256].astype(BF), tail], axis=0)
            v = mm(to8[...], v)
            for i in range(4):
                for j in range(8):
                    r = 64 * i + 8 * j
                    att[j, 4 * k + i] = v[r : r + 8, :].astype(BF)


def spatial_bwd(d_ref, q_ref, k_ref, v_ref, p_ref, ws, from8, keep7, out, datt, dq, dk, dv):
    h = pl.program_id(0)

    @pl.when(h == 0)
    def _():
        dq[...] = jnp.zeros_like(dq)
        dk[...] = jnp.zeros_like(dk)
        dv[...] = jnp.zeros_like(dv)
        lanes = lax.broadcasted_iota(jnp.int32, (T, 128), 1)
        for k in range(4):
            rows = slice(k * T, (k + 1) * T)
            v = [d_ref[j, 4 * k + i].astype(F32) for i in range(4) for j in range(8)]
            v = mm(from8[...], jnp.concatenate(v, axis=0).astype(BF))
            datt[rows, 0:256] = v[0:T, :]
            tail = v[T : 2 * T, :] * keep7[...].astype(F32)
            tail = tail[:, 0:128] + tail[:, 128:256]
            tail = tail + pltpu.roll(tail, 32, 1)
            tail = tail + pltpu.roll(tail, 64, 1)
            datt[rows, 256:384] = jnp.where(lanes < 32, tail, 0.0)

    start = pl.multiple_of((h // 2) * 128, 128)
    win = pl.ds(start, 256)
    first = HD * h - start
    lane = lax.broadcasted_iota(jnp.int32, (1, 256), 1)
    keep = (lane >= first) & (lane < first + HD)
    vwin = v_ref[:, win]
    kwin = jnp.where(keep, k_ref[:, win], 0)
    for i in range(4):
        rows = slice(i * T, (i + 1) * T)
        di = jnp.where(keep, datt[rows, win], 0.0).astype(BF)
        qi = jnp.where(keep, q_ref[rows, win], 0)
        pb = p_ref[0, rows, :]
        p = pb.astype(F32)
        dp = mm_nt(di, vwin)
        delta = jnp.sum(dp * p, axis=1, keepdims=True)
        ds = (p * ((dp - delta) * SCALE)).astype(BF)
        dq[rows, win] += mm(ds, kwin)
        dk[:, win] += mm_tn(ds, qi)
        dv[:, win] += mm_tn(pb, di)

    @pl.when(h == 3)
    def _():
        for k in range(4):
            rows = slice(k * T, (k + 1) * T)
            tail = (
                dq[rows, 256:384]
                + pltpu.roll(dk[rows, 256:384], 32, 1)
                + pltpu.roll(dv[rows, 256:384], 64, 1)
            )
            a = jnp.concatenate([dq[rows, 0:256], dk[rows, 0:256]], axis=1).astype(BF)
            b = jnp.concatenate([dv[rows, 0:256], tail], axis=1).astype(BF)
            out[rows, :] = (mm_nt(a, ws[0]) + mm_nt(b, ws[1, :, 128:512])).astype(BF)


def rows64(v):
    return v.astype(F32).reshape(64, v.shape[-1])


def temporal_kernel(pos, att, *refs):
    lus, consts, refs = refs[:8], refs[8:13], refs[13:]
    collect, share, keep8, body, fold = consts
    mod, wg, grad, datt, w0, w1, lu, qkv, dout, dqkv, sems = refs
    second = pltpu.make_async_copy(wg.at[pl.ds(D, D), pl.ds(128, 2816)], w1, sems.at[1])
    first = pltpu.make_async_copy(wg.at[pl.ds(0, D), :], w0, sems.at[0])
    second.start()
    first.start()
    n = 256
    for k in range(8):
        lu[lax.rem(pos[0] + 8 - k, 8)] = lus[k][...]
    lat = jnp.concatenate([rows64(lu[:, f, 0]) for f in range(4)], axis=0)
    up = jnp.concatenate([rows64(lu[:, f, 1]) for f in range(4)], axis=0)
    second.wait()
    branch = jnp.zeros((n, D), F32)
    tails = jnp.zeros((n, 128), F32)
    for g in range(4):
        a = jnp.concatenate([rows64(att[:, 4 * f + g]) for f in range(4)], axis=0).astype(BF)
        tail = mm(share[...], a).astype(BF) * keep8[...]
        tails += mm(tail, fold[g])
        branch += mm(a * body[...], w1[g * GW : g * GW + 256, 1664:2816])
    last = jnp.concatenate([w1[g * GW + 256 : (g + 1) * GW, 1664:2816] for g in range(4)], axis=0)
    branch += mm(tails.astype(BF), last)
    x = (lat + mod[2:3, :] * branch).astype(BF).astype(F32)
    hat, _ = normed(x)
    m = (hat * (1.0 + mod[4:5, :]) + mod[3:4, :]).astype(BF)
    gated = (up * mod[5:6, :]).astype(BF)
    dout[...] = mm_nt(gated, w1[:, 512:1664]).astype(BF)
    qkv[:, 2944:3456] = mm(m, w1[:, 0:512]).astype(BF)
    first.wait()
    qkv[:, 0:2944] = mm(m, w0[...]).astype(BF)
    dqkv[...] = jnp.zeros_like(dqkv)
    ri = lax.broadcasted_iota(jnp.int32, (n, n), 0)
    ci = lax.broadcasted_iota(jnp.int32, (n, n), 1)
    same = (ri & 7) == (ci & 7)
    lane = lax.broadcasted_iota(jnp.int32, (1, 256), 1)
    for h in range(16):
        start = min(128 * (HD * h // 128), D - 256)
        first_lane = HD * h - start
        keep = (lane >= first_lane) & (lane < first_lane + HD)
        qw = slice(start, start + 256)
        kw = slice(D + start, D + start + 256)
        vw = slice(2 * D + start, 2 * D + start + 256)
        q = jnp.where(keep, qkv[:, qw], 0)
        k = jnp.where(keep, qkv[:, kw], 0)
        v = qkv[:, vw]
        d = jnp.where(keep, dout[:, qw], 0)
        s = jnp.where(same, mm_nt(q, k) * (SCALE * LOG2E), -1e30)
        e = jnp.exp2(s - jnp.max(s, axis=1, keepdims=True))
        e = jnp.where(same, e, 0.0)
        p = e * (1.0 / jnp.sum(e, axis=1, keepdims=True))
        pb = p.astype(BF)
        dp = mm_nt(d, v)
        delta = jnp.sum(dp * p, axis=1, keepdims=True)
        ds = (p * ((dp - delta) * SCALE)).astype(BF)
        dqkv[:, qw] += mm(ds, k)
        dqkv[:, kw] += mm_tn(ds, q)
        dqkv[:, vw] += mm_tn(pb, d)
    dm = mm_nt(dqkv[:, 0:2944].astype(BF), w0[...])
    dm += mm_nt(dqkv[:, 2944:3456].astype(BF), w1[:, 0:512])
    through = norm_back(dm.astype(BF), x, mod[4:5, :])
    gh = (up + through.astype(F32)).astype(BF).astype(F32)
    for f in range(4):
        for j in range(8):
            r = 64 * f + 8 * j
            grad[lax.rem(8 + j - pos[0], 8), f] = gh[r : r + 8, :].astype(BF)
    gated = (gh * mod[2:3, :]).astype(BF)
    tails = mm_nt(gated, last).astype(BF)
    for g in range(4):
        r = mm_nt(gated, w1[g * GW : g * GW + 256, 1664:2816]) * body[...].astype(F32)
        tail = mm_nt(tails, fold[g]).astype(BF) * keep8[...]
        r += mm(collect[...], tail)
        for f in range(4):
            datt[:, 4 * f + g] = r[64 * f : 64 * f + 64, :].reshape(8, 8, 256).astype(BF)


def close_kernel(pos, dm_ref, l0, l1, mod, from8, *refs):
    ghs, own, other, gh = refs[:8], refs[8], refs[9], refs[10]
    for k in range(8):
        gh[lax.rem(pos[0] + 8 - k, 8)] = ghs[k][...]
    v = [gh[j, f].astype(F32) for f in range(4) for j in range(8)]
    v = mm(from8[0:T, :], jnp.concatenate(v, axis=0).astype(BF))
    for f in range(4):
        dm = sum(dm_ref[4 * f + g].astype(F32) for g in range(4))
        src = (l0 if f < 2 else l1)[f % 2].astype(F32)
        through = norm_back(dm.astype(BF), src, mod[1:2, :])
        total = v[f * HP : (f + 1) * HP, :] + through.astype(F32)
        (own if f < 2 else other)[f % 2] = total.astype(BF)


def pick(v, i):
    return lax.dynamic_index_in_dim(v, i, 0, keepdims=False)


def move(v, axis, n, k):
    if k % n == 0:
        return v
    return lax.ppermute(v, axis, [(i, (i + k) % n) for i in range(n)])


def a2a(v, axes):
    return lax.all_to_all(v, axes, split_axis=0, concat_axis=0, tiled=True)


def after(v, *others):
    return lax.optimization_barrier((v,) + others)[0]


def shards(latent, upstream, modulation, spatial_qkv, spatial_out, temporal_qkv, temporal_out):
    z, c, x, y = (lax.axis_index(a) for a in ("z", "c", "x", "y"))
    pos = jnp.stack([z, c, x, y]).astype(jnp.int32)
    mod = pick(modulation, c)
    swap = lambda v: lax.ppermute(v, "c", [(0, 1), (1, 0)])
    space = ("x", "y")

    l_own = pick(latent, c)
    l_other = swap(pick(latent, 1 - c))

    first = call(first_kernel, sds((16, ROWS, D)), [SM] + [VM] * 4)(
        pos, l_own, l_other, mod, spatial_qkv
    )
    got = a2a(first, space)

    wide = jnp.concatenate([after(temporal_qkv, first), temporal_out, spatial_out], axis=1)
    wide = lax.dynamic_slice_in_dim(wide, c * 2816, 2944, axis=1)
    wg = lax.all_gather(wide, ("c", "x", "y"), axis=0, tiled=True)

    up = after(upstream, first)
    sorted_ = call(sort_kernel, sds((8, 4, 2, 8, D)), [SM] + [VM] * 5)(
        pos, l_own, l_other, pick(up, c), swap(pick(up, 1 - c)), TO8
    )
    lus = [move(sorted_[k], "z", 8, k) for k in range(8)]
    got = after(got, *lus)
    wb = swap(got[:, HP:ROWS, :])

    whole = lambda *shape: pl.BlockSpec(shape, lambda h: (0,) * len(shape))
    pspec = pl.BlockSpec((1, 896, 896), lambda h: (h, 0, 0))
    att, q, k, v, probs, ws = pl.pallas_call(
        spatial_fwd,
        grid=(4,),
        in_specs=[SM, whole(16, ROWS, D), whole(16, 32, D), whole(256, 2 * T), whole(T, 256)],
        out_specs=[whole(8, 16, 8, 256)] + [whole(896, GP)] * 3 + [pspec, whole(2, D, 512)],
        out_shape=[sds((8, 16, 8, 256))]
        + [sds((896, GP))] * 3
        + [sds((4, 896, 896)), sds((2, D, 512))],
        scratch_shapes=[pltpu.VMEM((896, GP), F32)],
        compiler_params=pltpu.CompilerParams(vmem_limit_bytes=BIG),
    )(pos, got, wb, TO8, KEEP7)
    att_t = a2a(att.reshape(128, 8, 256), ("z", "x", "y")).reshape(8, 16, 8, 256)

    grad_t, datt = call(
        temporal_kernel,
        (sds((8, 4, 8, D)), sds((8, 16, 8, 256))),
        [SM] + [VM] * 15 + [HBM],
        [
            pltpu.VMEM((D, 2944), BF),
            pltpu.VMEM((D, 2816), BF),
            pltpu.VMEM((8, 4, 2, 8, D), BF),
            pltpu.VMEM((256, 3 * D), BF),
            pltpu.VMEM((256, D), BF),
            pltpu.VMEM((256, 3 * D), F32),
            pltpu.SemaphoreType.DMA((2,)),
        ],
    )(pos, att_t, *lus, COLLECT, SHARE, KEEP8, BODY, FOLD, mod, wg)

    datt_s = a2a(datt.reshape(128, 8, 256), ("z", "x", "y")).reshape(8, 16, 8, 256)

    partial = pl.pallas_call(
        spatial_bwd,
        grid=(4,),
        in_specs=[whole(8, 16, 8, 256)] + [whole(896, GP)] * 3 + [pspec, whole(2, D, 512), whole(2 * T, 256), whole(T, 256)],
        out_specs=whole(896, D),
        out_shape=sds((896, D)),
        scratch_shapes=[pltpu.VMEM((896, GP), F32)] * 4,
        compiler_params=pltpu.CompilerParams(vmem_limit_bytes=BIG),
    )(datt_s, q, k, v, probs, ws, FROM8, KEEP7)
    dm = a2a(partial.reshape(16, HP, D), space)
    grad_t = after(grad_t, partial)
    ghs = [move(grad_t[k], "z", 8, k) for k in range(8)]

    own, other = call(
        close_kernel,
        (sds((2, HP, D)),) * 2,
        [SM] + [VM] * 13,
        [pltpu.VMEM((8, 4, 8, D), BF)],
    )(pos, dm, l_own, l_other, mod, FROM8, *ghs)
    other = swap(other)
    return jnp.where(c == 0, jnp.stack([own, other]), jnp.stack([other, own]))


def solution(mesh):
    split = Mesh(mesh.devices.reshape(8, 2, 4, 4), ("z", "c", "x", "y"))
    tokens = P(None, ("z", "c"), ("x", "y"), None)
    rows = P(("x", "y"), None)
    return jax.shard_map(
        shards,
        mesh=split,
        in_specs=(tokens, tokens, P(), rows, rows, rows, rows),
        out_specs=tokens,
        check_vma=False,
    )
```

```python
import jax
import jax.numpy as jnp
import ml_dtypes
import numpy as np
from jax import lax
from jax.experimental import pallas as pl
from jax.experimental.pallas import tpu as pltpu
from jax.sharding import Mesh, PartitionSpec as P

HD = 72
EPS = 1e-06
D = 1152
GW = 288
GP = 384
T = 224
ROWS = 88
HP = 56
BIG = 60 * 2**20
BF = jnp.bfloat16
F32 = jnp.float32
LOG2E = 1.4426950408889634
SCALE = HD ** (-0.5)

def _tables():
    row7, row8, lane = np.arange(T), np.arange(256), np.arange(256)
    spread7 = (row8[:, None] // 8 == row7[None] // 7) & (row8[:, None] % 8 == row7[None] % 7)
    collect7 = (row8[:, None] // 8 == row7[None] // 7) & (row8[:, None] % 8 == 7)
    collect8 = (row8[:, None] // 8 == row8[None] // 8) & (row8[:, None] % 8 == 7)
    keep7 = row7[:, None] % 7 == lane[None] // 32
    keep8 = (row8[:, None] % 8 == lane[None] // 32) & (row8[:, None] % 8 < 7)
    body8 = np.broadcast_to(row8[:, None] % 8 < 7, (256, 256))
    fold = np.stack([lane[:, None] % 32 + 32 * g == np.arange(128)[None] for g in range(4)])
    to8 = np.concatenate([spread7, collect7], axis=1)
    return tuple(
        np.asarray(t, dtype=ml_dtypes.bfloat16)
        for t in (to8, to8.T, collect8, collect8.T, keep7, keep8, body8, fold)
    )


TO8, FROM8, COLLECT, SHARE, KEEP7, KEEP8, BODY, FOLD = _tables()

VM = pl.BlockSpec(memory_space=pltpu.VMEM)
SM = pl.BlockSpec(memory_space=pltpu.SMEM)
HBM = pl.BlockSpec(memory_space=pl.ANY)


def sds(shape, dtype=BF):
    return jax.ShapeDtypeStruct(shape, dtype)


def call(body, outs, n_in_specs, scratch=(), **kw):
    return pl.pallas_call(
        body,
        out_shape=outs,
        in_specs=n_in_specs,
        out_specs=jax.tree.map(lambda _: VM, outs),
        scratch_shapes=list(scratch),
        compiler_params=pltpu.CompilerParams(vmem_limit_bytes=BIG),
        **kw,
    )


def mm(a, b):
    return jnp.dot(a, b, preferred_element_type=F32)


def mm_nt(a, b):
    return lax.dot_general(a, b, (((1,), (1,)), ((), ())), preferred_element_type=F32)


def mm_tn(a, b):
    return lax.dot_general(a, b, (((0,), (0,)), ((), ())), preferred_element_type=F32)


def normed(x):
    centre = jnp.mean(x, axis=-1, keepdims=True)
    shifted = x - centre
    rstd = lax.rsqrt(jnp.mean(jnp.square(shifted), axis=-1, keepdims=True) + EPS)
    return shifted * rstd, rstd


def norm_back(dm, x, scaling):
    hat, rstd = normed(x)
    dn = dm.astype(F32) * (1.0 + scaling)
    mean_dn = jnp.mean(dn, axis=-1, keepdims=True)
    mean_hat = jnp.mean(dn * hat, axis=-1, keepdims=True)
    return (rstd * (dn - mean_dn - hat * mean_hat)).astype(BF)


def rows_of(lats):
    return jnp.concatenate([r[...].astype(F32) for r in lats], axis=0)


def first_kernel(pos, own, other, mod, w, out):
    wide = w[...].astype(F32)
    first = pos[1] == 0
    for g in range(4):
        q, k, v = (wide[:, j * D + g * GW : j * D + (g + 1) * GW] for j in range(3))
        low = jnp.concatenate([q[:, 0:256], k[:, 0:256]], axis=1)
        tail = jnp.concatenate(
            [q[:, 256:GW], k[:, 256:GW], v[:, 256:GW], jnp.zeros((HD, 32), F32)], axis=1
        )
        high = jnp.concatenate([k[:, 128:256], v[:, 0:256], tail], axis=1)
        half = jnp.where(first, low, high)
        lines = [
            jnp.concatenate(
                [half[8 * r : 8 * r + 8, 128 * i : 128 * i + 128] for r in range(9)], axis=1
            )
            for i in range(4)
        ]
        lines = jnp.concatenate(lines, axis=0).astype(BF)
        for f in range(4):
            out[4 * f + g, HP:ROWS, :] = lines
    for f in range(4):
        src = own if f < 2 else other
        hat, _ = normed(src[pos[1], f % 2].astype(F32))
        m = (hat * (1.0 + mod[1:2, :]) + mod[0:1, :]).astype(BF)
        for g in range(4):
            out[4 * f + g, 0:HP, :] = m


def sort_kernel(pos, l0, l1, u0, u1, to8, out):
    for i, pair in enumerate(((l0, l1), (u0, u1))):
        v = [src[pos[1], f].astype(F32) for src in pair for f in range(2)]
        v = jnp.concatenate(v, axis=0).astype(BF)
        v = mm(to8[:, 0:T], v).astype(BF).astype(F32)
        for f in range(4):
            for j in range(8):
                r = 64 * f + 8 * j
                out[lax.rem(8 + j - pos[0], 8), f, i] = v[r : r + 8, :].astype(BF)


def tail_to(t6, j):
    lane = lax.broadcasted_iota(jnp.int32, t6.shape, 1)
    moved = t6 if j == 0 else pltpu.roll(t6, 128 - 32 * j, 1)
    return jnp.where(lane < 32, moved, 0.0)


def spatial_fwd(pos, m_ref, wb, to8, keep7, att, p_ref, *refs):
    kept, (q_ref, k_ref, v_ref, ws, acc, sems) = refs[:4], refs[4:]
    h = pl.program_id(0)
    copies = [
        pltpu.make_async_copy(src, dst, sems.at[i])
        for i, (src, dst) in enumerate(zip((q_ref, k_ref, v_ref, ws), kept))
    ]

    @pl.when(h == 0)
    def _():
        acc[...] = jnp.zeros_like(acc)
        for half, src, at in ((pos[1], m_ref, HP), (1 - pos[1], wb, 0)):
            for i in range(4):
                v = src[:, at + 8 * i : at + 8 * i + 8, :].astype(F32)
                v = [v[:, :, 128 * r : 128 * r + 128] for r in range(9)]
                v = jnp.concatenate(v, axis=1).reshape(D, 128)
                ws[half, :, 128 * i : 128 * i + 128] = v.astype(BF)
        for k in range(4):
            rows = slice(k * T, (k + 1) * T)
            m = [m_ref[4 * k + i, 0:HP, :].astype(F32) for i in range(4)]
            m = jnp.concatenate(m, axis=0).astype(BF)
            r0 = mm(m, ws[0])
            r1 = mm(m, ws[1, :, 128:512])
            t6 = r1[:, 256:384]
            q_ref[rows, 0:256] = r0[:, 0:256].astype(BF)
            q_ref[rows, 256:384] = tail_to(t6, 0).astype(BF)
            k_ref[rows, 0:256] = r0[:, 256:512].astype(BF)
            k_ref[rows, 256:384] = tail_to(t6, 1).astype(BF)
            v_ref[rows, 0:256] = r1[:, 0:256].astype(BF)
            v_ref[rows, 256:384] = tail_to(t6, 2).astype(BF)
        for copy in copies:
            copy.start()

    start = pl.multiple_of((h // 2) * 128, 128)
    win = pl.ds(start, 256)
    first = HD * h - start
    lane = lax.broadcasted_iota(jnp.int32, (1, 256), 1)
    keep = (lane >= first) & (lane < first + HD)
    kwin = k_ref[:, win]
    vwin = jnp.where(keep, v_ref[:, win], 0)
    for i in range(2):
        rows = slice(i * 2 * T, (i + 1) * 2 * T)
        qi = jnp.where(keep, q_ref[rows, win], 0)
        s = mm_nt(qi, kwin) * (SCALE * LOG2E)
        e = jnp.exp2(s - jnp.max(s, axis=1, keepdims=True))
        p = (e * (1.0 / jnp.sum(e, axis=1, keepdims=True))).astype(BF)
        p_ref[0, rows, :] = p
        acc[rows, win] += mm(p, vwin)

    @pl.when(h == 3)
    def _():
        for k in range(4):
            rows = slice(k * T, (k + 1) * T)
            tail = acc[rows, 256:384]
            tail = tail + pltpu.roll(tail, 32, 1)
            tail = tail + pltpu.roll(tail, 64, 1)
            tail = jnp.concatenate([tail, tail], axis=1).astype(BF) * keep7[...]
            v = jnp.concatenate([acc[rows, 0:256].astype(BF), tail], axis=0)
            v = mm(to8[...], v)
            for i in range(4):
                for j in range(8):
                    r = 64 * i + 8 * j
                    att[j, 4 * k + i] = v[r : r + 8, :].astype(BF)
        for copy in copies:
            copy.wait()


def spatial_bwd(d_ref, q_ref, k_ref, v_ref, p_ref, from8, keep7, wh, out, *refs):
    ws, outs, datt, dq, dk, dv, sems = refs
    h = pl.program_id(0)
    weights = pltpu.make_async_copy(wh, ws, sems.at[4])

    @pl.when(h == 0)
    def _():
        weights.start()
        dq[...] = jnp.zeros_like(dq)
        dk[...] = jnp.zeros_like(dk)
        dv[...] = jnp.zeros_like(dv)
        lanes = lax.broadcasted_iota(jnp.int32, (T, 128), 1)
        for k in range(4):
            rows = slice(k * T, (k + 1) * T)
            v = [d_ref[j, 4 * k + i].astype(F32) for i in range(4) for j in range(8)]
            v = mm(from8[...], jnp.concatenate(v, axis=0).astype(BF))
            datt[rows, 0:256] = v[0:T, :]
            tail = v[T : 2 * T, :] * keep7[...].astype(F32)
            tail = tail[:, 0:128] + tail[:, 128:256]
            tail = tail + pltpu.roll(tail, 32, 1)
            tail = tail + pltpu.roll(tail, 64, 1)
            datt[rows, 256:384] = jnp.where(lanes < 32, tail, 0.0)

    start = pl.multiple_of((h // 2) * 128, 128)
    win = pl.ds(start, 256)
    first = HD * h - start
    lane = lax.broadcasted_iota(jnp.int32, (1, 256), 1)
    keep = (lane >= first) & (lane < first + HD)
    vwin = v_ref[:, win]
    kwin = jnp.where(keep, k_ref[:, win], 0)
    for i in range(2):
        rows = slice(i * 2 * T, (i + 1) * 2 * T)
        di = jnp.where(keep, datt[rows, win], 0.0).astype(BF)
        qi = jnp.where(keep, q_ref[rows, win], 0)
        pb = p_ref[0, rows, :]
        p = pb.astype(F32)
        dp = mm_nt(di, vwin)
        delta = jnp.sum(dp * p, axis=1, keepdims=True)
        ds = (p * ((dp - delta) * SCALE)).astype(BF)
        dq[rows, win] += mm(ds, kwin)
        dk[:, win] += mm_tn(ds, qi)
        dv[:, win] += mm_tn(pb, di)

    @pl.when(h == 3)
    def _():
        weights.wait()
        copies = []
        for k in range(4):
            rows = slice(k * T, (k + 1) * T)
            tail = (
                dq[rows, 256:384]
                + pltpu.roll(dk[rows, 256:384], 32, 1)
                + pltpu.roll(dv[rows, 256:384], 64, 1)
            )
            a = jnp.concatenate([dq[rows, 0:256], dk[rows, 0:256]], axis=1).astype(BF)
            b = jnp.concatenate([dv[rows, 0:256], tail], axis=1).astype(BF)
            outs[rows, :] = (mm_nt(a, ws[0]) + mm_nt(b, ws[1, :, 128:512])).astype(BF)
            copies.append(pltpu.make_async_copy(outs.at[rows, :], out.at[rows, :], sems.at[k]))
            copies[k].start()
        for copy in copies:
            copy.wait()


def rows64(v):
    return v.astype(F32).reshape(64, v.shape[-1])


def temporal_kernel(pos, att, *refs):
    lus, consts, refs = refs[:8], refs[8:13], refs[13:]
    collect, share, keep8, body, fold = consts
    mod, wg, grad, datt, w0, w1, lu, qkv, dout, dqkv, sems = refs
    def part(i, at, size):
        return pltpu.make_async_copy(
            wg.at[pl.ds(D, D), pl.ds(128 + at, size)], w1.at[:, pl.ds(at, size)], sems.at[i]
        )

    third, second, first = part(3, 1664, D), part(2, 512, D), part(1, 0, 512)
    main = pltpu.make_async_copy(wg.at[pl.ds(0, D), :], w0, sems.at[0])
    third.start()
    second.start()
    first.start()
    main.start()
    n = 256
    for k in range(8):
        lu[lax.rem(pos[0] + 8 - k, 8)] = lus[k][...]
    lat = jnp.concatenate([rows64(lu[:, f, 0]) for f in range(4)], axis=0)
    up = jnp.concatenate([rows64(lu[:, f, 1]) for f in range(4)], axis=0)
    third.wait()
    branch = jnp.zeros((n, D), F32)
    tails = jnp.zeros((n, 128), F32)
    for g in range(4):
        a = jnp.concatenate([rows64(att[:, 4 * f + g]) for f in range(4)], axis=0).astype(BF)
        tail = mm(share[...], a).astype(BF) * keep8[...]
        tails += mm(tail, fold[g])
        branch += mm(a * body[...], w1[g * GW : g * GW + 256, 1664:2816])
    last = jnp.concatenate([w1[g * GW + 256 : (g + 1) * GW, 1664:2816] for g in range(4)], axis=0)
    branch += mm(tails.astype(BF), last)
    x = (lat + mod[2:3, :] * branch).astype(BF).astype(F32)
    hat, _ = normed(x)
    m = (hat * (1.0 + mod[4:5, :]) + mod[3:4, :]).astype(BF)
    gated = (up * mod[5:6, :]).astype(BF)
    second.wait()
    dout[...] = mm_nt(gated, w1[:, 512:1664]).astype(BF)
    first.wait()
    qkv[:, 2944:3456] = mm(m, w1[:, 0:512]).astype(BF)
    main.wait()
    qkv[:, 0:2944] = mm(m, w0[...]).astype(BF)
    dqkv[...] = jnp.zeros_like(dqkv)
    ri = lax.broadcasted_iota(jnp.int32, (n, n), 0)
    ci = lax.broadcasted_iota(jnp.int32, (n, n), 1)
    same = (ri & 7) == (ci & 7)
    lane = lax.broadcasted_iota(jnp.int32, (1, 256), 1)
    for h in range(16):
        start = min(128 * (HD * h // 128), D - 256)
        first_lane = HD * h - start
        keep = (lane >= first_lane) & (lane < first_lane + HD)
        qw = slice(start, start + 256)
        kw = slice(D + start, D + start + 256)
        vw = slice(2 * D + start, 2 * D + start + 256)
        q = jnp.where(keep, qkv[:, qw], 0)
        k = jnp.where(keep, qkv[:, kw], 0)
        v = qkv[:, vw]
        d = jnp.where(keep, dout[:, qw], 0)
        s = jnp.where(same, mm_nt(q, k) * (SCALE * LOG2E), -1e30)
        e = jnp.exp2(s - jnp.max(s, axis=1, keepdims=True))
        p = e * (1.0 / jnp.sum(e, axis=1, keepdims=True))
        pb = p.astype(BF)
        dp = mm_nt(d, v)
        delta = jnp.sum(dp * p, axis=1, keepdims=True)
        ds = (p * ((dp - delta) * SCALE)).astype(BF)
        dqkv[:, qw] += mm(ds, k)
        dqkv[:, kw] += mm_tn(ds, q)
        dqkv[:, vw] += mm_tn(pb, d)
    dm = mm_nt(dqkv[:, 0:2944].astype(BF), w0[...])
    dm += mm_nt(dqkv[:, 2944:3456].astype(BF), w1[:, 0:512])
    through = norm_back(dm.astype(BF), x, mod[4:5, :])
    gh = (up + through.astype(F32)).astype(BF).astype(F32)
    for f in range(4):
        for j in range(8):
            r = 64 * f + 8 * j
            grad[lax.rem(8 + j - pos[0], 8), f] = gh[r : r + 8, :].astype(BF)
    gated = (gh * mod[2:3, :]).astype(BF)
    tails = mm_nt(gated, last).astype(BF)
    for g in range(4):
        r = mm_nt(gated, w1[g * GW : g * GW + 256, 1664:2816]) * body[...].astype(F32)
        tail = mm_nt(tails, fold[g]).astype(BF) * keep8[...]
        r += mm(collect[...], tail)
        for f in range(4):
            datt[:, 4 * f + g] = r[64 * f : 64 * f + 64, :].reshape(8, 8, 256).astype(BF)


def close_kernel(pos, dm_ref, l0, l1, mod, from8, *refs):
    ghs, own, other, gh = refs[:8], refs[8], refs[9], refs[10]
    for k in range(8):
        gh[lax.rem(pos[0] + 8 - k, 8)] = ghs[k][...]
    v = [gh[j, f].astype(F32) for f in range(4) for j in range(8)]
    v = mm(from8[0:T, :], jnp.concatenate(v, axis=0).astype(BF))
    for f in range(4):
        dm = sum(dm_ref[4 * f + g].astype(F32) for g in range(4))
        src = (l0 if f < 2 else l1)[pos[1], f % 2].astype(F32)
        through = norm_back(dm.astype(BF), src, mod[1:2, :])
        total = v[f * HP : (f + 1) * HP, :] + through.astype(F32)
        (own if f < 2 else other)[f % 2] = total.astype(BF)


def pick(v, i):
    return lax.dynamic_index_in_dim(v, i, 0, keepdims=False)


def move(v, axis, n, k):
    if k % n == 0:
        return v
    return lax.ppermute(v, axis, [(i, (i + k) % n) for i in range(n)])


def a2a(v, axes):
    return lax.all_to_all(v, axes, split_axis=0, concat_axis=0, tiled=True)


def after(v, *others):
    return lax.optimization_barrier((v,) + others)[0]


def shards(latent, upstream, modulation, spatial_qkv, spatial_out, temporal_qkv, temporal_out):
    z, c, x, y = (lax.axis_index(a) for a in ("z", "c", "x", "y"))
    pos = jnp.stack([z, c, x, y]).astype(jnp.int32)
    mod = pick(modulation, c)
    swap = lambda v: lax.ppermute(v, "c", [(0, 1), (1, 0)])
    space = ("x", "y")

    swapped = swap(latent)

    first = call(first_kernel, sds((16, ROWS, D)), [SM] + [VM] * 4)(
        pos, latent, swapped, mod, spatial_qkv
    )
    got = a2a(first, space)

    wide = jnp.concatenate([after(temporal_qkv, first), temporal_out, spatial_out], axis=1)
    wide = lax.dynamic_slice_in_dim(wide, c * 2816, 2944, axis=1)
    wg = lax.all_gather(wide, ("c", "x", "y"), axis=0, tiled=True)

    up = after(upstream, first)
    sorted_ = call(sort_kernel, sds((8, 4, 2, 8, D)), [SM] + [VM] * 5)(
        pos, latent, swapped, up, swap(up), TO8
    )
    lus = [move(sorted_[k], "z", 8, k) for k in range(8)]
    got = after(got, *lus)
    wb = swap(got[:, HP:ROWS, :])

    whole = lambda *shape: pl.BlockSpec(shape, lambda h: (0,) * len(shape))
    pspec = pl.BlockSpec((1, 896, 896), lambda h: (h, 0, 0))
    att, probs, q, k, v, ws = pl.pallas_call(
        spatial_fwd,
        grid=(4,),
        in_specs=[SM, whole(16, ROWS, D), whole(16, 32, D), whole(256, 2 * T), whole(T, 256)],
        out_specs=[whole(8, 16, 8, 256), pspec] + [HBM] * 4,
        out_shape=[sds((8, 16, 8, 256)), sds((4, 896, 896))]
        + [sds((896, GP))] * 3
        + [sds((2, D, 512))],
        scratch_shapes=[pltpu.VMEM((896, GP), BF)] * 3
        + [
            pltpu.VMEM((2, D, 512), BF),
            pltpu.VMEM((896, GP), F32),
            pltpu.SemaphoreType.DMA((4,)),
        ],
        compiler_params=pltpu.CompilerParams(vmem_limit_bytes=BIG),
    )(pos, got, wb, TO8, KEEP7)
    att_t = a2a(att.reshape(128, 8, 256), ("z", "x", "y")).reshape(8, 16, 8, 256)

    grad_t, datt = call(
        temporal_kernel,
        (sds((8, 4, 8, D)), sds((8, 16, 8, 256))),
        [SM] + [VM] * 15 + [HBM],
        [
            pltpu.VMEM((D, 2944), BF),
            pltpu.VMEM((D, 2816), BF),
            pltpu.VMEM((8, 4, 2, 8, D), BF),
            pltpu.VMEM((256, 3 * D), BF),
            pltpu.VMEM((256, D), BF),
            pltpu.VMEM((256, 3 * D), F32),
            pltpu.SemaphoreType.DMA((4,)),
        ],
    )(pos, att_t, *lus, COLLECT, SHARE, KEEP8, BODY, FOLD, mod, wg)

    datt_s = a2a(datt.reshape(128, 8, 256), ("z", "x", "y")).reshape(8, 16, 8, 256)

    partial = pl.pallas_call(
        spatial_bwd,
        grid=(4,),
        in_specs=[whole(8, 16, 8, 256)]
        + [whole(896, GP)] * 3
        + [pspec, whole(2 * T, 256), whole(T, 256), HBM],
        out_specs=HBM,
        out_shape=sds((896, D)),
        scratch_shapes=[pltpu.VMEM((2, D, 512), BF), pltpu.VMEM((896, D), BF)]
        + [pltpu.VMEM((896, GP), F32)] * 4
        + [pltpu.SemaphoreType.DMA((5,))],
        compiler_params=pltpu.CompilerParams(vmem_limit_bytes=BIG),
    )(datt_s, q, k, v, probs, FROM8, KEEP7, ws)
    dm = a2a(partial.reshape(16, HP, D), space)
    grad_t = after(grad_t, partial)
    ghs = [move(grad_t[k], "z", 8, k) for k in range(8)]

    own, other = call(
        close_kernel,
        (sds((2, HP, D)),) * 2,
        [SM] + [VM] * 13,
        [pltpu.VMEM((8, 4, 8, D), BF)],
    )(pos, dm, latent, swapped, mod, FROM8, *ghs)
    other = swap(other)
    return jnp.where(c == 0, jnp.stack([own, other]), jnp.stack([other, own]))


def solution(mesh):
    split = Mesh(mesh.devices.reshape(8, 2, 4, 4), ("z", "c", "x", "y"))
    tokens = P(None, ("z", "c"), ("x", "y"), None)
    rows = P(("x", "y"), None)
    return jax.shard_map(
        shards,
        mesh=split,
        in_specs=(tokens, tokens, P(), rows, rows, rows, rows),
        out_specs=tokens,
        check_vma=False,
    )
```

```python
import jax
import jax.numpy as jnp
import ml_dtypes
import numpy as np
from jax import lax
from jax.experimental import pallas as pl
from jax.experimental.pallas import tpu as pltpu
from jax.sharding import Mesh, PartitionSpec as P

HD = 72
EPS = 1e-06
D = 1152
GW = 288
GP = 384
T = 224
ROWS = 88
HP = 56
BIG = 60 * 2**20
BF = jnp.bfloat16
F32 = jnp.float32
LOG2E = 1.4426950408889634
SCALE = HD ** (-0.5)

def _tables():
    row7, row8, lane = np.arange(T), np.arange(256), np.arange(256)
    spread7 = (row8[:, None] // 8 == row7[None] // 7) & (row8[:, None] % 8 == row7[None] % 7)
    collect7 = (row8[:, None] // 8 == row7[None] // 7) & (row8[:, None] % 8 == 7)
    collect8 = (row8[:, None] // 8 == row8[None] // 8) & (row8[:, None] % 8 == 7)
    keep7 = row7[:, None] % 7 == lane[None] // 32
    keep8 = (row8[:, None] % 8 == lane[None] // 32) & (row8[:, None] % 8 < 7)
    body8 = np.broadcast_to(row8[:, None] % 8 < 7, (256, 256))
    fold = np.stack([lane[:, None] % 32 + 32 * g == np.arange(128)[None] for g in range(4)])
    to8 = np.concatenate([spread7, collect7], axis=1)
    return tuple(
        np.asarray(t, dtype=ml_dtypes.bfloat16)
        for t in (to8, to8.T, collect8, collect8.T, keep7, keep8, body8, fold)
    )


TO8, FROM8, COLLECT, SHARE, KEEP7, KEEP8, BODY, FOLD = _tables()

VM = pl.BlockSpec(memory_space=pltpu.VMEM)
SM = pl.BlockSpec(memory_space=pltpu.SMEM)
HBM = pl.BlockSpec(memory_space=pl.ANY)


def sds(shape, dtype=BF):
    return jax.ShapeDtypeStruct(shape, dtype)


def call(body, outs, n_in_specs, scratch=(), **kw):
    return pl.pallas_call(
        body,
        out_shape=outs,
        in_specs=n_in_specs,
        out_specs=jax.tree.map(lambda _: VM, outs),
        scratch_shapes=list(scratch),
        compiler_params=pltpu.CompilerParams(vmem_limit_bytes=BIG),
        **kw,
    )


def mm(a, b):
    return jnp.dot(a, b, preferred_element_type=F32)


def mm_nt(a, b):
    return lax.dot_general(a, b, (((1,), (1,)), ((), ())), preferred_element_type=F32)


def mm_tn(a, b):
    return lax.dot_general(a, b, (((0,), (0,)), ((), ())), preferred_element_type=F32)


def normed(x):
    centre = jnp.mean(x, axis=-1, keepdims=True)
    shifted = x - centre
    rstd = lax.rsqrt(jnp.mean(jnp.square(shifted), axis=-1, keepdims=True) + EPS)
    return shifted * rstd, rstd


def norm_back(dm, x, scaling):
    hat, rstd = normed(x)
    dn = dm.astype(F32) * (1.0 + scaling)
    mean_dn = jnp.mean(dn, axis=-1, keepdims=True)
    mean_hat = jnp.mean(dn * hat, axis=-1, keepdims=True)
    return (rstd * (dn - mean_dn - hat * mean_hat)).astype(BF)


def rows_of(lats):
    return jnp.concatenate([r[...].astype(F32) for r in lats], axis=0)


def first_kernel(pos, own, other, mod, w, out):
    wide = w[...].astype(F32)
    first = pos[1] == 0
    for g in range(4):
        q, k, v = (wide[:, j * D + g * GW : j * D + (g + 1) * GW] for j in range(3))
        low = jnp.concatenate([q[:, 0:256], k[:, 0:256]], axis=1)
        tail = jnp.concatenate(
            [q[:, 256:GW], k[:, 256:GW], v[:, 256:GW], jnp.zeros((HD, 32), F32)], axis=1
        )
        high = jnp.concatenate([k[:, 128:256], v[:, 0:256], tail], axis=1)
        half = jnp.where(first, low, high)
        lines = [
            jnp.concatenate(
                [half[8 * r : 8 * r + 8, 128 * i : 128 * i + 128] for r in range(9)], axis=1
            )
            for i in range(4)
        ]
        lines = jnp.concatenate(lines, axis=0).astype(BF)
        for f in range(4):
            out[4 * f + g, HP:ROWS, :] = lines
    for f in range(4):
        src = own if f < 2 else other
        hat, _ = normed(src[pos[1], f % 2].astype(F32))
        m = (hat * (1.0 + mod[1:2, :]) + mod[0:1, :]).astype(BF)
        for g in range(4):
            out[4 * f + g, 0:HP, :] = m


def sort_kernel(pos, l0, l1, u0, u1, to8, out):
    for i, pair in enumerate(((l0, l1), (u0, u1))):
        v = [src[pos[1], f].astype(F32) for src in pair for f in range(2)]
        v = jnp.concatenate(v, axis=0).astype(BF)
        v = mm(to8[:, 0:T], v).astype(BF).astype(F32)
        for f in range(4):
            for j in range(8):
                r = 64 * f + 8 * j
                out[lax.rem(8 + j - pos[0], 8), f, i] = v[r : r + 8, :].astype(BF)


def tail_to(t6, j):
    lane = lax.broadcasted_iota(jnp.int32, t6.shape, 1)
    moved = t6 if j == 0 else pltpu.roll(t6, 128 - 32 * j, 1)
    return jnp.where(lane < 32, moved, 0.0)


def spatial_fwd(pos, m_ref, wb, to8, keep7, att, p_ref, *refs):
    kept, (q_ref, k_ref, v_ref, ws, acc, sems) = refs[:4], refs[4:]
    h = pl.program_id(0)
    copies = [
        pltpu.make_async_copy(src, dst, sems.at[i])
        for i, (src, dst) in enumerate(zip((q_ref, k_ref, v_ref, ws), kept))
    ]

    @pl.when(h == 0)
    def _():
        acc[...] = jnp.zeros_like(acc)
        for half, src, at in ((pos[1], m_ref, HP), (1 - pos[1], wb, 0)):
            for i in range(4):
                v = src[:, at + 8 * i : at + 8 * i + 8, :].astype(F32)
                v = [v[:, :, 128 * r : 128 * r + 128] for r in range(9)]
                v = jnp.concatenate(v, axis=1).reshape(D, 128)
                ws[half, :, 128 * i : 128 * i + 128] = v.astype(BF)
        for k in range(4):
            rows = slice(k * T, (k + 1) * T)
            m = [m_ref[4 * k + i, 0:HP, :].astype(F32) for i in range(4)]
            m = jnp.concatenate(m, axis=0).astype(BF)
            r0 = mm(m, ws[0])
            r1 = mm(m, ws[1, :, 128:512])
            t6 = r1[:, 256:384]
            q_ref[rows, 0:256] = r0[:, 0:256].astype(BF)
            q_ref[rows, 256:384] = tail_to(t6, 0).astype(BF)
            k_ref[rows, 0:256] = r0[:, 256:512].astype(BF)
            k_ref[rows, 256:384] = tail_to(t6, 1).astype(BF)
            v_ref[rows, 0:256] = r1[:, 0:256].astype(BF)
            v_ref[rows, 256:384] = tail_to(t6, 2).astype(BF)
        for copy in copies:
            copy.start()

    start = pl.multiple_of((h // 2) * 128, 128)
    win = pl.ds(start, 256)
    first = HD * h - start
    lane = lax.broadcasted_iota(jnp.int32, (1, 256), 1)
    keep = (lane >= first) & (lane < first + HD)
    kwin = k_ref[:, win]
    vwin = jnp.where(keep, v_ref[:, win], 0)
    for i in range(2):
        rows = slice(i * 2 * T, (i + 1) * 2 * T)
        qi = jnp.where(keep, q_ref[rows, win], 0)
        s = mm_nt(qi, kwin) * (SCALE * LOG2E)
        e = jnp.exp2(s - jnp.max(s, axis=1, keepdims=True))
        p = (e * (1.0 / jnp.sum(e, axis=1, keepdims=True))).astype(BF)
        p_ref[0, rows, :] = p
        acc[rows, win] += mm(p, vwin)

    @pl.when(h == 3)
    def _():
        for k in range(4):
            rows = slice(k * T, (k + 1) * T)
            tail = acc[rows, 256:384]
            tail = tail + pltpu.roll(tail, 32, 1)
            tail = tail + pltpu.roll(tail, 64, 1)
            tail = jnp.concatenate([tail, tail], axis=1).astype(BF) * keep7[...]
            v = jnp.concatenate([acc[rows, 0:256].astype(BF), tail], axis=0)
            v = mm(to8[...], v)
            for i in range(4):
                for j in range(8):
                    r = 64 * i + 8 * j
                    att[j, 4 * k + i] = v[r : r + 8, :].astype(BF)
        for copy in copies:
            copy.wait()


def spatial_bwd(d_ref, q_ref, k_ref, v_ref, p_ref, from8, keep7, wh, out, *refs):
    ws, outs, datt, dq, dk, dv, sems = refs
    h = pl.program_id(0)
    weights = pltpu.make_async_copy(wh, ws, sems.at[4])

    @pl.when(h == 0)
    def _():
        weights.start()
        dq[...] = jnp.zeros_like(dq)
        dk[...] = jnp.zeros_like(dk)
        dv[...] = jnp.zeros_like(dv)
        lanes = lax.broadcasted_iota(jnp.int32, (T, 128), 1)
        for k in range(4):
            rows = slice(k * T, (k + 1) * T)
            v = [d_ref[j, 4 * k + i].astype(F32) for i in range(4) for j in range(8)]
            v = mm(from8[...], jnp.concatenate(v, axis=0).astype(BF))
            datt[rows, 0:256] = v[0:T, :]
            tail = v[T : 2 * T, :] * keep7[...].astype(F32)
            tail = tail[:, 0:128] + tail[:, 128:256]
            tail = tail + pltpu.roll(tail, 32, 1)
            tail = tail + pltpu.roll(tail, 64, 1)
            datt[rows, 256:384] = jnp.where(lanes < 32, tail, 0.0)

    start = pl.multiple_of((h // 2) * 128, 128)
    win = pl.ds(start, 256)
    first = HD * h - start
    lane = lax.broadcasted_iota(jnp.int32, (1, 256), 1)
    keep = (lane >= first) & (lane < first + HD)
    vwin = v_ref[:, win]
    kwin = jnp.where(keep, k_ref[:, win], 0)
    for i in range(2):
        rows = slice(i * 2 * T, (i + 1) * 2 * T)
        di = jnp.where(keep, datt[rows, win], 0.0).astype(BF)
        qi = jnp.where(keep, q_ref[rows, win], 0)
        pb = p_ref[0, rows, :]
        p = pb.astype(F32)
        dp = mm_nt(di, vwin)
        delta = jnp.sum(dp * p, axis=1, keepdims=True)
        ds = (p * ((dp - delta) * SCALE)).astype(BF)
        dq[rows, win] += mm(ds, kwin)
        dk[:, win] += mm_tn(ds, qi)
        dv[:, win] += mm_tn(pb, di)

    @pl.when(h == 3)
    def _():
        weights.wait()
        copies = []
        for k in range(4):
            rows = slice(k * T, (k + 1) * T)
            tail = (
                dq[rows, 256:384]
                + pltpu.roll(dk[rows, 256:384], 32, 1)
                + pltpu.roll(dv[rows, 256:384], 64, 1)
            )
            a = jnp.concatenate([dq[rows, 0:256], dk[rows, 0:256]], axis=1).astype(BF)
            b = jnp.concatenate([dv[rows, 0:256], tail], axis=1).astype(BF)
            outs[rows, :] = (mm_nt(a, ws[0]) + mm_nt(b, ws[1, :, 128:512])).astype(BF)
            copies.append(pltpu.make_async_copy(outs.at[rows, :], out.at[rows, :], sems.at[k]))
            copies[k].start()
        for copy in copies:
            copy.wait()


def rows64(v):
    return v.astype(F32).reshape(64, v.shape[-1])


def temporal_kernel(pos, att, *refs):
    lus, consts, refs = refs[:8], refs[8:13], refs[13:]
    collect, share, keep8, body, fold = consts
    mod, wg, grad, datt, w0, w1, lu, qkv, dout, dqkv, sems = refs
    def part(i, at, size):
        return pltpu.make_async_copy(
            wg.at[pl.ds(D, D), pl.ds(128 + at, size)], w1.at[:, pl.ds(at, size)], sems.at[i]
        )

    third, second, first = part(3, 1664, D), part(2, 512, D), part(1, 0, 512)
    main = pltpu.make_async_copy(wg.at[pl.ds(0, D), :], w0, sems.at[0])
    third.start()
    second.start()
    first.start()
    main.start()
    n = 256
    for k in range(8):
        lu[lax.rem(pos[0] + 8 - k, 8)] = lus[k][...]
    lat = jnp.concatenate([rows64(lu[:, f, 0]) for f in range(4)], axis=0)
    up = jnp.concatenate([rows64(lu[:, f, 1]) for f in range(4)], axis=0)
    third.wait()
    branch = jnp.zeros((n, D), F32)
    tails = jnp.zeros((n, 128), F32)
    for g in range(4):
        a = jnp.concatenate([rows64(att[:, 4 * f + g]) for f in range(4)], axis=0).astype(BF)
        tail = mm(share[...], a).astype(BF) * keep8[...]
        tails += mm(tail, fold[g])
        branch += mm(a * body[...], w1[g * GW : g * GW + 256, 1664:2816])
    last = jnp.concatenate([w1[g * GW + 256 : (g + 1) * GW, 1664:2816] for g in range(4)], axis=0)
    branch += mm(tails.astype(BF), last)
    x = (lat + mod[2:3, :] * branch).astype(BF).astype(F32)
    hat, _ = normed(x)
    m = (hat * (1.0 + mod[4:5, :]) + mod[3:4, :]).astype(BF)
    gated = (up * mod[5:6, :]).astype(BF)
    second.wait()
    dout[...] = mm_nt(gated, w1[:, 512:1664]).astype(BF)
    first.wait()
    qkv[:, 2944:3456] = mm(m, w1[:, 0:512]).astype(BF)
    main.wait()
    qkv[:, 0:2944] = mm(m, w0[...]).astype(BF)
    dqkv[...] = jnp.zeros_like(dqkv)
    ri = lax.broadcasted_iota(jnp.int32, (n, n), 0)
    ci = lax.broadcasted_iota(jnp.int32, (n, n), 1)
    same = (ri & 7) == (ci & 7)
    lane = lax.broadcasted_iota(jnp.int32, (1, 256), 1)
    for h in range(16):
        start = min(128 * (HD * h // 128), D - 256)
        first_lane = HD * h - start
        keep = (lane >= first_lane) & (lane < first_lane + HD)
        qw = slice(start, start + 256)
        kw = slice(D + start, D + start + 256)
        vw = slice(2 * D + start, 2 * D + start + 256)
        q = jnp.where(keep, qkv[:, qw], 0)
        k = jnp.where(keep, qkv[:, kw], 0)
        v = qkv[:, vw]
        d = jnp.where(keep, dout[:, qw], 0)
        s = jnp.where(same, mm_nt(q, k) * (SCALE * LOG2E), -1e30)
        e = jnp.exp2(s - jnp.max(s, axis=1, keepdims=True))
        p = e * (1.0 / jnp.sum(e, axis=1, keepdims=True))
        pb = p.astype(BF)
        dp = mm_nt(d, v)
        delta = jnp.sum(dp * p, axis=1, keepdims=True)
        ds = (p * ((dp - delta) * SCALE)).astype(BF)
        dqkv[:, qw] += mm(ds, k)
        dqkv[:, kw] += mm_tn(ds, q)
        dqkv[:, vw] += mm_tn(pb, d)
    dm = mm_nt(dqkv[:, 0:2944].astype(BF), w0[...])
    dm += mm_nt(dqkv[:, 2944:3456].astype(BF), w1[:, 0:512])
    through = norm_back(dm.astype(BF), x, mod[4:5, :])
    gh = (up + through.astype(F32)).astype(BF).astype(F32)
    for f in range(4):
        for j in range(8):
            r = 64 * f + 8 * j
            grad[lax.rem(8 + j - pos[0], 8), f] = gh[r : r + 8, :].astype(BF)
    gated = (gh * mod[2:3, :]).astype(BF)
    tails = mm_nt(gated, last).astype(BF)
    for g in range(4):
        r = mm_nt(gated, w1[g * GW : g * GW + 256, 1664:2816]) * body[...].astype(F32)
        tail = mm_nt(tails, fold[g]).astype(BF) * keep8[...]
        r += mm(collect[...], tail)
        for f in range(4):
            datt[:, 4 * f + g] = r[64 * f : 64 * f + 64, :].reshape(8, 8, 256).astype(BF)


def close_kernel(pos, dm_ref, l0, l1, mod, from8, *refs):
    ghs, out, other, gh = refs[:8], refs[8], refs[9], refs[10]
    for k in range(8):
        gh[lax.rem(pos[0] + 8 - k, 8)] = ghs[k][...]
    v = [gh[j, f].astype(F32) for f in range(4) for j in range(8)]
    v = mm(from8[0:T, :], jnp.concatenate(v, axis=0).astype(BF))
    for f in range(4):
        dm = sum(dm_ref[4 * f + g].astype(F32) for g in range(4))
        src = (l0 if f < 2 else l1)[pos[1], f % 2].astype(F32)
        through = norm_back(dm.astype(BF), src, mod[1:2, :])
        total = v[f * HP : (f + 1) * HP, :] + through.astype(F32)
        if f < 2:
            out[pos[1], f] = total.astype(BF)
        else:
            other[f - 2] = total.astype(BF)


def pick(v, i):
    return lax.dynamic_index_in_dim(v, i, 0, keepdims=False)


def move(v, axis, n, k):
    if k % n == 0:
        return v
    return lax.ppermute(v, axis, [(i, (i + k) % n) for i in range(n)])


def a2a(v, axes):
    return lax.all_to_all(v, axes, split_axis=0, concat_axis=0, tiled=True)


def after(v, *others):
    return lax.optimization_barrier((v,) + others)[0]


def shards(latent, upstream, modulation, spatial_qkv, spatial_out, temporal_qkv, temporal_out):
    z, c, x, y = (lax.axis_index(a) for a in ("z", "c", "x", "y"))
    pos = jnp.stack([z, c, x, y]).astype(jnp.int32)
    mod = pick(modulation, c)
    swap = lambda v: lax.ppermute(v, "c", [(0, 1), (1, 0)])
    space = ("x", "y")

    swapped = swap(latent)

    first = call(first_kernel, sds((16, ROWS, D)), [SM] + [VM] * 4)(
        pos, latent, swapped, mod, spatial_qkv
    )
    got = a2a(first, space)

    wide = jnp.concatenate([after(temporal_qkv, first), temporal_out, spatial_out], axis=1)
    wide = lax.dynamic_slice_in_dim(wide, c * 2816, 2944, axis=1)
    wg = lax.all_gather(wide, ("c", "x", "y"), axis=0, tiled=True)

    up = after(upstream, first)
    sorted_ = call(sort_kernel, sds((8, 4, 2, 8, D)), [SM] + [VM] * 5)(
        pos, latent, swapped, up, swap(up), TO8
    )
    lus = [move(sorted_[k], "z", 8, k) for k in range(8)]
    got = after(got, *lus)
    wb = swap(got[:, HP:ROWS, :])

    whole = lambda *shape: pl.BlockSpec(shape, lambda h: (0,) * len(shape))
    pspec = pl.BlockSpec((1, 896, 896), lambda h: (h, 0, 0))
    att, probs, q, k, v, ws = pl.pallas_call(
        spatial_fwd,
        grid=(4,),
        in_specs=[SM, whole(16, ROWS, D), whole(16, 32, D), whole(256, 2 * T), whole(T, 256)],
        out_specs=[whole(8, 16, 8, 256), pspec] + [HBM] * 4,
        out_shape=[sds((8, 16, 8, 256)), sds((4, 896, 896))]
        + [sds((896, GP))] * 3
        + [sds((2, D, 512))],
        scratch_shapes=[pltpu.VMEM((896, GP), BF)] * 3
        + [
            pltpu.VMEM((2, D, 512), BF),
            pltpu.VMEM((896, GP), F32),
            pltpu.SemaphoreType.DMA((4,)),
        ],
        compiler_params=pltpu.CompilerParams(vmem_limit_bytes=BIG),
    )(pos, got, wb, TO8, KEEP7)
    att_t = a2a(att.reshape(128, 8, 256), ("z", "x", "y")).reshape(8, 16, 8, 256)

    grad_t, datt = call(
        temporal_kernel,
        (sds((8, 4, 8, D)), sds((8, 16, 8, 256))),
        [SM] + [VM] * 15 + [HBM],
        [
            pltpu.VMEM((D, 2944), BF),
            pltpu.VMEM((D, 2816), BF),
            pltpu.VMEM((8, 4, 2, 8, D), BF),
            pltpu.VMEM((256, 3 * D), BF),
            pltpu.VMEM((256, D), BF),
            pltpu.VMEM((256, 3 * D), F32),
            pltpu.SemaphoreType.DMA((4,)),
        ],
    )(pos, att_t, *lus, COLLECT, SHARE, KEEP8, BODY, FOLD, mod, wg)

    datt_s = a2a(datt.reshape(128, 8, 256), ("z", "x", "y")).reshape(8, 16, 8, 256)

    partial = pl.pallas_call(
        spatial_bwd,
        grid=(4,),
        in_specs=[whole(8, 16, 8, 256)]
        + [whole(896, GP)] * 3
        + [pspec, whole(2 * T, 256), whole(T, 256), HBM],
        out_specs=HBM,
        out_shape=sds((896, D)),
        scratch_shapes=[pltpu.VMEM((2, D, 512), BF), pltpu.VMEM((896, D), BF)]
        + [pltpu.VMEM((896, GP), F32)] * 4
        + [pltpu.SemaphoreType.DMA((5,))],
        compiler_params=pltpu.CompilerParams(vmem_limit_bytes=BIG),
    )(datt_s, q, k, v, probs, FROM8, KEEP7, ws)
    dm = a2a(partial.reshape(16, HP, D), space)
    grad_t = after(grad_t, partial)
    ghs = [move(grad_t[k], "z", 8, k) for k in range(8)]

    out, other = call(
        close_kernel,
        (sds((2, 2, HP, D)), sds((2, HP, D))),
        [SM] + [VM] * 13,
        [pltpu.VMEM((8, 4, 8, D), BF)],
    )(pos, dm, latent, swapped, mod, FROM8, *ghs)
    return lax.dynamic_update_slice(out, swap(other)[None], (1 - c, 0, 0, 0))


def solution(mesh):
    split = Mesh(mesh.devices.reshape(8, 2, 4, 4), ("z", "c", "x", "y"))
    tokens = P(None, ("z", "c"), ("x", "y"), None)
    rows = P(("x", "y"), None)
    return jax.shard_map(
        shards,
        mesh=split,
        in_specs=(tokens, tokens, P(), rows, rows, rows, rows),
        out_specs=tokens,
        check_vma=False,
    )
```
